512 devices in a mesh: cube: 4 (over x), row: 8 (over y), col: 16 (over z, core).
Axes of the slice: x: 4, y: 8, z: 8, core: 2. Of those that a mesh axis runs over, the one named last changes fastest.
Arguments:
- front_tiles: float32 [3, 32, 256, 2, 16, 256], P(None, ('cube', 'row'), None, None, 'col'), may hold values from -1 to 64, as said below
- child_tiles: bfloat16 [4, 8, 16, 4, 256, 256], P('cube', 'row', 'col'), may hold values from -0.5 to 0.5
- target_rows: int32 [4, 8, 16, 4], P('cube', 'row', 'col'), may hold values from 0 to 95, as said below
- target_cols: int32 [4, 8, 16, 4], P('cube', 'row', 'col'), may hold values from 0 to 31, as said below
- live_counts: int32 [4, 8, 16], P('cube', 'row', 'col'), may hold values from 1 to 4, as said below
Outputs:
- factored: float32 [3, 32, 256, 2, 16, 256], P(None, ('cube', 'row'), None, None, 'col')
The draws below stay inside these ranges and needn't reach their ends.
Inputs may be any that keep to these rules, and one draw needn't show every extreme that they name: `live_counts`: some device holds 4 live slots in every draw. target_rows[c, r, q, m] leaves remainder r on division by the row axis's size. Call the owning cube index of a parent tile row its remainder modulo 32, divided by the row axis's size: of one device's live slots at most 2 have one owning cube index, and in every draw some owner receives 2 live slots from every device that shares its row and col indices. target_cols[c, r, q, m] leaves remainder q on division by 16. `front_tiles`: after assembly the symmetric part of tile (0, 0) is positive definite.
All inputs are finite; a program needn't handle non-finite values.
Results may differ from the reference program's by a relative error of at most 0.0003.
Values may be sent and summed in bfloat16 or wider, within the bound.
A program may use at most 64 MiB of HBM per device.

```python
import jax
import jax.numpy as jnp
from jax import lax

TILE = 256
FT = 96
TC_DEV = 2
CS = 4
MOST = 2
GRID_ROWS = 32
GRID_COLS = 16
TR = 3
WT = 32
N_CUBE = 4
N_ROW = 8
N_COL = 16


def slot_plan(key):
    owners = N_CUBE * N_ROW
    lane_total = N_CUBE * MOST
    keys = jax.random.split(key, 7)
    grid_shape = (N_CUBE, N_ROW, N_COL)
    scores = jax.random.randint(keys[0], grid_shape + (lane_total,), 0, 1 << 20) * lane_total + jnp.arange(lane_total, dtype=jnp.int32)
    ordering = jnp.argsort(scores, axis=-1)[..., :CS]
    dest_cube = ordering // MOST
    chosen_row = jax.random.randint(keys[1], (), 0, N_ROW)
    chosen_col = jax.random.randint(keys[2], (), 0, N_COL)
    chosen_cube = jax.random.randint(keys[3], (), 0, N_CUBE)
    in_group = (jnp.arange(N_ROW)[None, :, None] == chosen_row) & (jnp.arange(N_COL)[None, None, :] == chosen_col)
    slot_ids = jnp.arange(CS, dtype=jnp.int32)
    forced = jnp.where(slot_ids < MOST, chosen_cube, (chosen_cube + 1 + (slot_ids - MOST) // MOST) % N_CUBE)
    dest_cube = jnp.where(in_group[..., None], forced[None, None, None, :], dest_cube)
    counts = jax.random.randint(keys[4], grid_shape, 1, CS + 1)
    counts = jnp.where(in_group, CS, counts)
    local_row = jax.random.randint(keys[5], grid_shape + (CS,), 0, TR)
    local_col = jax.random.randint(keys[6], grid_shape + (CS,), 0, TC_DEV)
    row_index = jnp.arange(N_ROW, dtype=jnp.int32)[None, :, None, None]
    col_index = jnp.arange(N_COL, dtype=jnp.int32)[None, None, :, None]
    parent_rows = local_row * owners + dest_cube * N_ROW + row_index
    parent_cols = local_col * N_COL + col_index
    return (parent_rows.astype(jnp.int32), parent_cols.astype(jnp.int32), counts.astype(jnp.int32))


def draw_target_rows(key, part):
    return slot_plan(key)[0]


def draw_target_cols(key, part):
    return slot_plan(key)[1]


def draw_live_counts(key, part):
    return slot_plan(key)[2]


def draw_front_tiles(key, part):
    key = jax.random.fold_in(key, 11)
    keys = jax.random.split(key, 2)
    owners = N_CUBE * N_ROW
    full_shape = (TR, owners, TILE, TC_DEV, N_COL, TILE)
    offdiag = jax.random.uniform(keys[0], full_shape, jnp.float32, -1.0, 1.0)
    tile_row = (jnp.arange(TR)[:, None] * owners + jnp.arange(owners)[None, :])[:, :, None, None, None, None]
    tile_col = (jnp.arange(TC_DEV)[:, None] * N_COL + jnp.arange(N_COL)[None, :])[None, None, None, :, :, None]
    inner_row = jnp.arange(TILE)[None, None, :, None, None, None]
    inner_col = jnp.arange(TILE)[None, None, None, None, None, :]
    on_diagonal = (tile_row == tile_col) & (inner_row == inner_col)
    base_lift = float(TILE // 8 + 16)
    lift_spread = float(TILE // 16)
    lifted = base_lift + jax.random.uniform(keys[1], full_shape, jnp.float32, 0.0, lift_spread)
    return jnp.where(on_diagonal, lifted, offdiag)


def level_of(rng, dims, cuts, least, high):
    def one(position, blocks):
        steps = jax.random.uniform(jax.random.fold_in(jax.random.fold_in(rng, 6), position), (blocks,), jnp.float32, least / len(cuts), high / len(cuts))
        return jnp.repeat(jnp.exp(steps), dims[position] // blocks).reshape((-1,) + (1,) * (len(dims) - position - 1))

    loudness = one(*cuts[0])
    for cut in cuts[1:]:
        loudness = loudness * one(*cut)
    return loudness


def setup_inputs(seed: int = 0) -> dict:
    streams_of = jax.random.split(jax.random.key(seed), 6)
    return {
        "front_tiles": draw_front_tiles(jax.random.fold_in(streams_of[5], 71), 0),
        "child_tiles": jnp.clip(jax.random.uniform(streams_of[1], (N_CUBE, N_ROW, N_COL, CS, TILE, TILE), jnp.float32, -0.5, 0.5) * level_of(streams_of[1], (N_CUBE, N_ROW, N_COL, CS, TILE, TILE), ((0, 4), (1, 8), (2, 16)), -0.4, 0.0), -0.5, 0.5).astype(jnp.bfloat16),
        "target_rows": draw_target_rows(jax.random.fold_in(streams_of[5], 71), 0),
        "target_cols": draw_target_cols(jax.random.fold_in(streams_of[5], 71), 0),
        "live_counts": draw_live_counts(jax.random.fold_in(streams_of[5], 71), 0),
    }


HIGHEST_PREC = lax.Precision.HIGHEST

def reference(front_tiles, child_tiles, target_rows, target_cols, live_counts):
    tile_stack = front_tiles.reshape(FT, TILE, WT, TILE).transpose(0, 2, 1, 3).reshape(FT * WT, TILE, TILE)
    slot_ids = jnp.arange(CS, dtype=jnp.int32)
    slot_alive = (slot_ids[None, None, None, :] < live_counts[..., None]).astype(jnp.float32)
    slot_terms = child_tiles.astype(jnp.float32) * slot_alive[..., None, None]
    dest_index = (target_rows * WT + target_cols).astype(jnp.int32).reshape(-1)
    tile_stack = tile_stack.at[dest_index].add(slot_terms.reshape(-1, TILE, TILE))
    assembled = tile_stack.reshape(FT, WT, TILE, TILE)
    corner = assembled[0, 0]
    factor = jnp.linalg.cholesky(0.5 * (corner + corner.T))
    first_column = assembled[:, 0]
    solved = lax.linalg.triangular_solve(jnp.broadcast_to(factor, first_column.shape), first_column, left_side=False, lower=True, transpose_a=True)
    global_rows = jnp.arange(FT, dtype=jnp.int32)
    panel_tiles = jnp.where(global_rows[:, None, None] == 0, factor[None], solved)
    update = jnp.einsum('iab,jcb->ijac', panel_tiles, panel_tiles[:WT], precision=HIGHEST_PREC)
    global_cols = jnp.arange(WT, dtype=jnp.int32)
    trailing = assembled - update
    result = jnp.where(global_cols[None, :, None, None] == 0, panel_tiles[:, None], jnp.where(global_rows[:, None, None, None] == 0, jnp.zeros_like(trailing), trailing))
    return result.transpose(0, 2, 1, 3).reshape(TR, GRID_ROWS, TILE, TC_DEV, GRID_COLS, TILE)
```

```python
import jax
import jax.numpy as jnp
from jax import lax
from jax.experimental import pallas as pl
from jax.experimental.pallas import tpu as pltpu
from jax.sharding import PartitionSpec as P

MESH = pl.DeviceIdType.MESH
HIGHEST = lax.Precision.HIGHEST
F32 = jnp.float32
BF16 = jnp.bfloat16

NX, NY, NZ = 4, 8, 8
OWNERS = NX * NY
NCOL = 2 * NZ
TILE = 256
TR = 3
SLOTS = 4
LANES = 2
META = LANES * TILE
STAGE_ROWS = META + 16
PIECE = TILE // OWNERS
ZPIECE = TILE // NZ
NB = 32
NCHUNK = TILE // NB


def nt(a, b):
    return lax.dot_general(a, b, (((1,), (1,)), ((), ())), precision=HIGHEST, preferred_element_type=F32)


def drain(view, sem, times=1):
    for _ in range(times):
        pltpu.make_async_copy(view, view, sem).wait()


def cholesky_step(b, m_ref, u_ref, w_ref):
    row0 = pl.multiple_of(b * NB, NB)
    block = m_ref[pl.ds(row0, NB), :]
    half = jnp.where(b < NCHUNK // 2, block[:, :128], block[:, 128:256])
    diag = pltpu.roll(half, lax.rem(128 - lax.rem(b * NB, 128), 128), 1)
    parts = [block[:, 128 * i : 128 * (i + 1)] for i in range(4)] + [diag]
    rows = lax.broadcasted_iota(jnp.int32, (NB, 128), 0)
    for g in range(NB // 8):
        base = 8 * g
        cols = [jnp.broadcast_to(parts[4][base:, base + j : base + j + 1], (NB - base, 128)) for j in range(8)]
        live = [p[base:] for p in parts]
        below = rows[base:] - base
        for kk in range(8):
            pivot = cols[kk][kk : kk + 1, :]
            inv = lax.rsqrt(pivot)
            inv = inv * (1.5 - 0.5 * pivot * inv * inv)
            col = cols[kk] * inv
            masked = jnp.where(below > kk, col, 0.0)
            for j in range(kk + 1, 8):
                cols[j] = cols[j] - masked * col[j : j + 1, :]
            for i in range(5):
                top = live[i][kk : kk + 1, :] * inv
                live[i] = jnp.where(below == kk, top, live[i] - masked * top)
        parts = [l if g == 0 else jnp.concatenate([p[:base], l], axis=0) for p, l in zip(parts, live)]
    u = jnp.concatenate(parts[:2], axis=1)
    winv = jnp.concatenate(parts[2:4], axis=1)
    u_ref[pl.ds(row0, NB), :] = u
    w_ref[pl.ds(row0, NB), :] = winv
    both = jnp.concatenate(parts[:4], axis=1)
    b1 = both.astype(BF16)
    rest = both - b1.astype(F32)
    b2 = rest.astype(BF16)
    b3 = (rest - b2.astype(F32)).astype(BF16)
    a1, a2, a3 = b1[:, :TILE], b2[:, :TILE], b3[:, :TILE]
    lhs = jnp.concatenate([a1, a1, a2, a2, a1, a3], axis=0)
    rhs = jnp.concatenate([b1, b2, b1, b2, b3, b1], axis=0)
    m_ref[...] -= lax.dot_general(lhs, rhs, (((0,), (0,)), ((), ())), preferred_element_type=F32)


def kernel(
    front, child, trow, tcol, live, out,
    stage, recv, asm, brow, bcol, w, m_ref, u_ref,
    ch_s, ch_r, cs_s, cs_r, ca_s, ca_r, rs_s, rs_r, ra_s, ra_r, rf_s, rf_r, w_s, w_r,
):
    x, y, q = lax.axis_index("cube"), lax.axis_index("row"), lax.axis_index("col")
    z, h = q // 2, q % 2
    k = x * NY + y
    is_root = (k == 0) & (q == 0)
    is_helper = (k == 0) & (q == 1)

    def at(xx, yy, zz, hh):
        return (xx, yy, zz * 2 + hh)

    def send(src, dst, ssem, rsem, device):
        pltpu.make_async_remote_copy(
            src_ref=src, dst_ref=dst, send_sem=ssem, recv_sem=rsem, device_id=device, device_id_type=MESH
        ).start()

    my_s, my_q = k // NCOL, k % NCOL
    my_z, my_h = my_q // 2, my_q % 2

    barrier = pltpu.get_barrier_semaphore()

    def greet(device):
        pl.semaphore_signal(barrier, inc=1, device_id=device, device_id_type=MESH)

    def greet_plane(i, c):
        p = lax.rem(k + i, OWNERS)
        greet(at(p // NY, lax.rem(p, NY), z, h))
        return c

    def greet_z(i, c):
        greet(at(x, y, lax.rem(z + i, NZ), h))
        return c

    lax.fori_loop(1, NX * NY, greet_plane, 0)
    lax.fori_loop(1, NZ, greet_z, 0)
    greet(at(x, y, z, 1 - h))

    for s in range(2):
        owner = s * NCOL + q
        @pl.when((owner != 0) & jnp.logical_not((owner == k) & (q == 0)))
        def _():
            greet(at(owner // NY, lax.rem(owner, NY), 0, 0))

    alive = [jnp.where(m < live[0], 1, 0) for m in range(SLOTS)]
    cube_of = [lax.rem(trow[m], OWNERS) // NY for m in range(SLOTS)]
    tile_of = [(trow[m] // OWNERS) * 2 + tcol[m] // NCOL for m in range(SLOTS)]
    meta_row = lax.broadcasted_iota(jnp.int32, (16, TILE), 0)
    for d in range(NX):
        seen = 0
        index = [0, 0]
        label = [-1, -1]
        for m in range(SLOTS):
            hit = alive[m] * jnp.where(cube_of[m] == d, 1, 0)
            for lane in range(LANES):
                here = hit * jnp.where(seen == lane, 1, 0)
                index[lane] = index[lane] + here * m
                label[lane] = label[lane] + here * (tile_of[m] + 1)
            seen = seen + hit
        for lane in range(LANES):
            stage[d, lane * TILE : (lane + 1) * TILE, :] = child[index[lane]]
        tags = jnp.where(meta_row == 0, label[0], jnp.where(meta_row == 1, label[1], -1))
        stage[d, META:, :] = tags.astype(F32).astype(BF16)

    w[: TILE // 2, TILE // 2 :] = jnp.zeros((TILE // 2, TILE // 2), F32)

    greeted_by_column = jnp.where((q != 0) | (k == 0), 0, jnp.where(k == NCOL, OWNERS - 1, OWNERS))
    pl.semaphore_wait(barrier, NX * NY - 1 + NZ - 1 + 1 + greeted_by_column)

    for i in range(1, NX):
        d = lax.rem(x + i, NX)
        send(stage.at[d], recv.at[x], ch_s.at[i], ch_r.at[x], at(d, y, z, h))
    recv[x] = stage[x]

    def wait_children():
        for i in range(1, NX):
            src = lax.rem(x + i, NX)
            drain(recv.at[src], ch_r.at[src])

    def assemble(t, s, dst):
        tile_id = (t * 2 + s).astype(F32) if hasattr(t, "astype") else float(t * 2 + s)
        masks = []
        for src in range(NX):
            tags = recv[src, META:, :].astype(F32)
            masks.append([tags[lane : lane + 1, :] == tile_id for lane in range(LANES)])

        def rows(i, c):
            r0 = pl.multiple_of(i * 32, 32)
            start = t * (TILE * 4) + i * 128 + 2 * s
            acc = jnp.concatenate(
                [front[pl.ds(start, 32, stride=4), :], front[pl.ds(start + 1, 32, stride=4), :]], axis=1
            )
            for src in range(NX):
                for lane in range(LANES):
                    v = recv[src, pl.ds(lane * TILE + r0, 32), :].astype(F32)
                    acc = acc + jnp.where(masks[src][lane], v, 0.0)
            dst[pl.ds(r0, 32), :] = acc
            return c

        lax.fori_loop(0, TILE // 32, rows, 0)

    @pl.when(q == 0)
    def _():
        wait_children()
        assemble(0, 0, brow.at[0])

        @pl.when(k != 0)
        def _():
            def scatter(p, c):
                view = pl.ds(pl.multiple_of(p * PIECE, PIECE), PIECE)
                @pl.when((p != k) | (my_q != 0))
                def _():
                    send(brow.at[0, view, :], bcol.at[my_s, view, :], cs_s, cs_r.at[my_s],
                         at(p // NY, lax.rem(p, NY), my_z, my_h))
                return c

            lax.fori_loop(0, OWNERS, scatter, 0)

        @pl.when(k == NCOL)
        def _():
            bcol[1, NCOL * PIECE : (NCOL + 1) * PIECE, :] = brow[0, NCOL * PIECE : (NCOL + 1) * PIECE, :]

        for t in range(1, TR):
            assemble(t, 0, brow.at[t])

        def spread(p, c):
            view = pl.ds(pl.multiple_of(p * ZPIECE, ZPIECE), ZPIECE)
            send(brow.at[:, view, :], brow.at[:, view, :], rs_s, rs_r, at(x, y, p, 0))
            send(brow.at[:, 0:ZPIECE, :], brow.at[:, 0:ZPIECE, :], ra_s, ra_r.at[0], at(x, y, p, 0))
            return c

        lax.fori_loop(1, NZ, spread, 0)
        send(brow, brow, rf_s, rf_r, at(x, y, 0, 1))

    @pl.when(is_root)
    def _():
        a = brow[0]
        m_ref[:, :TILE] = 0.5 * (a + a.T)
        ii = lax.broadcasted_iota(jnp.int32, (TILE, TILE), 0)
        jj = lax.broadcasted_iota(jnp.int32, (TILE, TILE), 1)
        m_ref[:, TILE:] = jnp.where(ii == jj, 1.0, 0.0)

        def narrow(b, c):
            cholesky_step(b, m_ref, u_ref, w)
            view = pl.ds(pl.multiple_of(b * NB, NB), NB)
            send(w.at[view, 0:128], w.at[view, 0:128], w_s, w_r.at[b], at(0, 0, 0, 1))
            return c

        def wide(b, c):
            cholesky_step(b, m_ref, u_ref, w)
            view = pl.ds(pl.multiple_of(b * NB, NB), NB)
            send(w.at[view, :], w.at[view, :], w_s, w_r.at[b], at(0, 0, 0, 1))
            return c

        lax.fori_loop(0, NCHUNK // 2, narrow, 0)
        lax.fori_loop(NCHUNK // 2, NCHUNK, wide, 0)

    @pl.when(q != 0)
    def _():
        drain(bcol.at[0, 0:PIECE, :], cs_r.at[0])

    @pl.when(jnp.logical_not((q == 0) & (k == NCOL)))
    def _():
        drain(bcol.at[0, 0:PIECE, :], cs_r.at[1])

    mine = pl.ds(pl.multiple_of(k * PIECE, PIECE), PIECE)

    def gather_columns(i, c):
        p = lax.rem(k + i, OWNERS)
        send(bcol.at[:, mine, :], bcol.at[:, mine, :], ca_s, ca_r, at(p // NY, lax.rem(p, NY), z, h))
        return c

    lax.fori_loop(1, OWNERS, gather_columns, 0)

    @pl.when((h == 0) & (z != 0))
    def _():
        drain(brow.at[:, 0:ZPIECE, :], rs_r)
        view = pl.ds(pl.multiple_of(z * ZPIECE, ZPIECE), ZPIECE)

        def gather_rows(i, c):
            to = lax.rem(z + i, NZ)
            @pl.when(to != 0)
            def _():
                send(brow.at[:, view, :], brow.at[:, view, :], ra_s, ra_r.at[z], at(x, y, to, 0))
            return c

        lax.fori_loop(1, NZ, gather_rows, 0)

    @pl.when(q != 0)
    def _():
        wait_children()

        def all_rows(t, c):
            assemble(t, 0, asm.at[0, t])
            return c

        lax.fori_loop(0, TR, all_rows, 0)

    def second_rows(t, c):
        assemble(t, 1, asm.at[1, t])
        return c

    lax.fori_loop(0, TR, second_rows, 0)

    @pl.when((h == 0) & (z != 0))
    def _():
        def one(i, c):
            frm = lax.rem(z + i, NZ)
            drain(brow.at[:, 0:ZPIECE, :], ra_r.at[frm])
            return c

        lax.fori_loop(1, NZ, one, 0)
        send(brow, brow, rf_s, rf_r, at(x, y, z, 1))

    def pass_on(b, part):
        @pl.when((k == 0) & (z == 0))
        def _():
            for i in range(1, NX):
                send(part, part, w_s, w_r.at[b], at(i, 0, 0, 1))

        @pl.when((y == 0) & (z == 0))
        def _():
            for i in range(1, NY):
                send(part, part, w_s, w_r.at[b], at(x, i, 0, 1))

        @pl.when(z == 0)
        def _():
            for i in range(1, NZ):
                send(part, part, w_s, w_r.at[b], at(x, y, i, 1))

        @pl.when(jnp.logical_not(is_helper))
        def _():
            send(part, part, w_s, w_r.at[b], at(x, y, z, 0))

    def narrow_part(b):
        return w.at[pl.ds(pl.multiple_of(b * NB, NB), NB), 0:128]

    def wide_part(b):
        return w.at[pl.ds(pl.multiple_of(b * NB, NB), NB), :]

    @pl.when(jnp.logical_not(is_root))
    def _():
        def narrow(b, c):
            drain(narrow_part(b), w_r.at[b])
            @pl.when(h == 1)
            def _():
                pass_on(b, narrow_part(b))
            return c

        def wide(b, c):
            drain(wide_part(b), w_r.at[b])
            @pl.when(h == 1)
            def _():
                pass_on(b, wide_part(b))
            return c

        lax.fori_loop(0, NCHUNK // 2, narrow, 0)
        lax.fori_loop(NCHUNK // 2, NCHUNK, wide, 0)

    drain(bcol.at[:, 0 : TILE - PIECE, :], ca_r)

    @pl.when(h == 1)
    def _():
        drain(brow, rf_r)

    winv = w[...]
    pcol = [nt(bcol[s], winv) for s in range(2)]

    def update(t, c):
        panel = nt(brow[t], winv)
        first = (k == 0) & (t == 0)
        for s in range(2):
            tile = asm[s, t] - nt(panel, pcol[s])
            tile = jnp.where(first, 0.0, tile)
            if s == 0:
                tile = jnp.where(q == 0, panel, tile)
            start = t * (TILE * 4) + 2 * s
            out[pl.ds(start, TILE, stride=4), :] = tile[:, :128]
            out[pl.ds(start + 1, TILE, stride=4), :] = tile[:, 128:]
        return c

    lax.fori_loop(0, TR, update, 0)

    @pl.when(is_root)
    def _():
        ii = lax.broadcasted_iota(jnp.int32, (TILE, TILE), 0)
        jj = lax.broadcasted_iota(jnp.int32, (TILE, TILE), 1)
        factor = jnp.where(ii >= jj, u_ref[...].T, 0.0)
        out[pl.ds(0, TILE, stride=4), :] = factor[:, :128]
        out[pl.ds(1, TILE, stride=4), :] = factor[:, 128:]

    for i in range(1, NX):
        drain(stage.at[0], ch_s.at[i])

    def each(count, view, sem):
        def one(i, c):
            drain(view, sem)
            return c
        lax.fori_loop(0, count, one, 0)

    @pl.when((q == 0) & (k != 0))
    def _():
        each(jnp.where(k == NCOL, OWNERS - 1, OWNERS), brow.at[0, 0:PIECE, :], cs_s)

    each(OWNERS - 1, bcol.at[:, 0:PIECE, :], ca_s)

    @pl.when(q == 0)
    def _():
        each(NZ - 1, brow.at[:, 0:ZPIECE, :], rs_s)
        each(NZ - 1, brow.at[:, 0:ZPIECE, :], ra_s)

    @pl.when((h == 0) & (z != 0))
    def _():
        each(NZ - 2, brow.at[:, 0:ZPIECE, :], ra_s)

    @pl.when(h == 0)
    def _():
        drain(brow, rf_s)

    sent = (
        jnp.where((h == 1) & (k == 0) & (z == 0), NX - 1, 0)
        + jnp.where((h == 1) & (y == 0) & (z == 0), NY - 1, 0)
        + jnp.where((h == 1) & (z == 0), NZ - 1, 0)
        + jnp.where((h == 1) & jnp.logical_not(is_helper), 1, 0)
        + jnp.where(is_root, 1, 0)
    )
    each(sent * (NCHUNK // 2), w.at[0:NB, 0:128], w_s)
    each(sent * (NCHUNK // 2), w.at[0:NB, :], w_s)


def local(front_tiles, child_tiles, target_rows, target_cols, live_counts):
    front = front_tiles.reshape(TR * TILE * 4, 128)
    child = child_tiles.reshape(SLOTS, TILE, TILE)
    vmem = pl.BlockSpec(memory_space=pltpu.VMEM)
    smem = pl.BlockSpec(memory_space=pltpu.SMEM)
    dma = pltpu.SemaphoreType.DMA
    out = pl.pallas_call(
        kernel,
        out_shape=jax.ShapeDtypeStruct(front.shape, F32),
        in_specs=[vmem, vmem, smem, smem, smem],
        out_specs=vmem,
        scratch_shapes=[
            pltpu.VMEM((NX, STAGE_ROWS, TILE), BF16),
            pltpu.VMEM((NX, STAGE_ROWS, TILE), BF16),
            pltpu.VMEM((2, TR, TILE, TILE), F32),
            pltpu.VMEM((TR, TILE, TILE), F32),
            pltpu.VMEM((2, TILE, TILE), F32),
            pltpu.VMEM((TILE, TILE), F32),
            pltpu.VMEM((TILE, 2 * TILE), F32),
            pltpu.VMEM((TILE, TILE), F32),
            dma((NX,)), dma((NX,)),
            dma, dma((2,)),
            dma, dma,
            dma, dma,
            dma, dma((NZ,)),
            dma, dma,
            dma, dma((NCHUNK,)),
        ],
        compiler_params=pltpu.CompilerParams(
            collective_id=0, has_side_effects=True, vmem_limit_bytes=48 * 1024 * 1024
        ),
        cost_estimate=pl.CostEstimate(flops=11 * 2 * TILE**3, bytes_accessed=4 * 1024 * 1024, transcendentals=0),
        name="front_panel",
    )(front, child, target_rows.reshape(SLOTS), target_cols.reshape(SLOTS), live_counts.reshape(1))
    return out.reshape(front_tiles.shape)


def solution(mesh):
    placed = (
        P(None, ("cube", "row"), None, None, "col", None),
        P("cube", "row", "col", None, None, None),
        P("cube", "row", "col", None),
        P("cube", "row", "col", None),
        P("cube", "row", "col"),
    )
    return jax.shard_map(
        local,
        mesh=mesh,
        in_specs=placed,
        out_specs=P(None, ("cube", "row"), None, None, "col", None),
        check_vma=False,
    )
```

```python
import jax
import jax.numpy as jnp
from jax import lax
from jax.experimental import pallas as pl
from jax.experimental.pallas import tpu as pltpu
from jax.sharding import PartitionSpec as P

MESH = pl.DeviceIdType.MESH
HIGHEST = lax.Precision.HIGHEST
F32 = jnp.float32
BF16 = jnp.bfloat16

NX, NY, NZ = 4, 8, 8
OWNERS = NX * NY
NCOL = 2 * NZ
TILE = 256
TR = 3
SLOTS = 4
LANES = 2
META = LANES * TILE
STAGE_ROWS = META + 16
PIECE = TILE // OWNERS
ZPIECE = TILE // NZ
NB = 32
NBLOCK = TILE // NB
CHUNKS = ((0, 128, 128), (128, 64, 256), (192, 32, 256), (224, 32, 256))
NCHUNK = len(CHUNKS)


def nt(a, b):
    return lax.dot_general(a, b, (((1,), (1,)), ((), ())), precision=HIGHEST, preferred_element_type=F32)


def drain(view, sem, times=1):
    for _ in range(times):
        pltpu.make_async_copy(view, view, sem).wait()


def cholesky_step(b, m_ref, u_ref, w_ref):
    row0 = pl.multiple_of(b * NB, NB)
    block = m_ref[pl.ds(row0, NB), :]
    half = jnp.where(b < NBLOCK // 2, block[:, :128], block[:, 128:256])
    diag = pltpu.roll(half, lax.rem(128 - lax.rem(b * NB, 128), 128), 1)
    parts = [block[:, 128 * i : 128 * (i + 1)] for i in range(4)] + [diag]
    rows = lax.broadcasted_iota(jnp.int32, (NB, 128), 0)
    for g in range(NB // 8):
        base = 8 * g
        cols = [jnp.broadcast_to(parts[4][base:, base + j : base + j + 1], (NB - base, 128)) for j in range(8)]
        live = [p[base:] for p in parts]
        below = rows[base:] - base
        for kk in range(8):
            pivot = cols[kk][kk : kk + 1, :]
            inv = lax.rsqrt(pivot)
            inv = inv * (1.5 - 0.5 * pivot * inv * inv)
            col = cols[kk] * inv
            masked = jnp.where(below > kk, col, 0.0)
            for j in range(kk + 1, 8):
                cols[j] = cols[j] - masked * col[j : j + 1, :]
            for i in range(5):
                top = live[i][kk : kk + 1, :] * inv
                live[i] = jnp.where(below == kk, top, live[i] - masked * top)
        parts = [l if g == 0 else jnp.concatenate([p[:base], l], axis=0) for p, l in zip(parts, live)]
    u = jnp.concatenate(parts[:2], axis=1)
    winv = jnp.concatenate(parts[2:4], axis=1)
    u_ref[pl.ds(row0, NB), :] = u
    w_ref[pl.ds(row0, NB), :] = winv
    both = jnp.concatenate(parts[:4], axis=1)
    b1 = both.astype(BF16)
    rest = both - b1.astype(F32)
    b2 = rest.astype(BF16)
    b3 = (rest - b2.astype(F32)).astype(BF16)
    a1, a2, a3 = b1[:, :TILE], b2[:, :TILE], b3[:, :TILE]
    lhs = jnp.concatenate([a1, a1, a2, a2, a1, a3], axis=0)
    rhs = jnp.concatenate([b1, b2, b1, b2, b3, b1], axis=0)
    m_ref[...] -= lax.dot_general(lhs, rhs, (((0,), (0,)), ((), ())), preferred_element_type=F32)


def kernel(
    front_h, child_h, trow_h, tcol_h, live_h, out,
    front, child, trow, tcol, live, in_s, stage, recv, asm, brow, bcol, w, m_ref, u_ref,
    ch_s, ch_r, cs_s, cs_r, ca_s, ca_r, rs_s, rs_r, ra_s, ra_r, rf_s, rf_r, w_s, w_r,
):
    x, y, q = lax.axis_index("cube"), lax.axis_index("row"), lax.axis_index("col")
    z, h = q // 2, q % 2
    k = x * NY + y
    is_root = (k == 0) & (q == 0)
    is_helper = (k == 0) & (q == 1)

    loads = [
        pltpu.make_async_copy(src, dst, in_s.at[i])
        for i, (src, dst) in enumerate(
            [(trow_h, trow), (tcol_h, tcol), (live_h, live), (child_h, child), (front_h, front)]
        )
    ]
    for load in loads:
        load.start()

    def at(xx, yy, zz, hh):
        return (xx, yy, zz * 2 + hh)

    def send(src, dst, ssem, rsem, device):
        pltpu.make_async_remote_copy(
            src_ref=src, dst_ref=dst, send_sem=ssem, recv_sem=rsem, device_id=device, device_id_type=MESH
        ).start()

    my_s, my_q = k // NCOL, k % NCOL
    my_z, my_h = my_q // 2, my_q % 2

    barrier = pltpu.get_barrier_semaphore()

    def greet(device):
        pl.semaphore_signal(barrier, inc=1, device_id=device, device_id_type=MESH)

    def greet_plane(i, c):
        p = lax.rem(k + i, OWNERS)
        greet(at(p // NY, lax.rem(p, NY), z, h))
        return c

    def greet_z(i, c):
        greet(at(x, y, lax.rem(z + i, NZ), h))
        return c

    lax.fori_loop(1, NX * NY, greet_plane, 0)
    lax.fori_loop(1, NZ, greet_z, 0)
    greet(at(x, y, z, 1 - h))

    for s in range(2):
        owner = s * NCOL + q
        @pl.when((owner != 0) & jnp.logical_not((owner == k) & (q == 0)))
        def _():
            greet(at(owner // NY, lax.rem(owner, NY), 0, 0))

    for load in loads[:4]:
        load.wait()
    alive = [jnp.where(m < live[0], 1, 0) for m in range(SLOTS)]
    cube_of = [lax.rem(trow[m], OWNERS) // NY for m in range(SLOTS)]
    tile_of = [(trow[m] // OWNERS) * 2 + tcol[m] // NCOL for m in range(SLOTS)]
    meta_row = lax.broadcasted_iota(jnp.int32, (16, TILE), 0)
    for d in range(NX):
        seen = 0
        index = [0, 0]
        label = [-1, -1]
        for m in range(SLOTS):
            hit = alive[m] * jnp.where(cube_of[m] == d, 1, 0)
            for lane in range(LANES):
                here = hit * jnp.where(seen == lane, 1, 0)
                index[lane] = index[lane] + here * m
                label[lane] = label[lane] + here * (tile_of[m] + 1)
            seen = seen + hit
        for lane in range(LANES):
            stage[d, lane * TILE : (lane + 1) * TILE, :] = child[index[lane]]
        tags = jnp.where(meta_row == 0, label[0], jnp.where(meta_row == 1, label[1], -1))
        stage[d, META:, :] = tags.astype(F32).astype(BF16)

    w[: TILE // 2, TILE // 2 :] = jnp.zeros((TILE // 2, TILE // 2), F32)

    loads[4].wait()
    greeted_by_column = jnp.where((q != 0) | (k == 0), 0, jnp.where(k == NCOL, OWNERS - 1, OWNERS))
    pl.semaphore_wait(barrier, NX * NY - 1 + NZ - 1 + 1 + greeted_by_column)

    for i in range(1, NX):
        d = lax.rem(x + i, NX)
        send(stage.at[d], recv.at[x], ch_s.at[i], ch_r.at[x], at(d, y, z, h))
    recv[x] = stage[x]

    def wait_children():
        for i in range(1, NX):
            src = lax.rem(x + i, NX)
            drain(recv.at[src], ch_r.at[src])

    def assemble(t, s, dst):
        tile_id = (t * 2 + s).astype(F32) if hasattr(t, "astype") else float(t * 2 + s)
        masks = []
        for src in range(NX):
            tags = recv[src, META:, :].astype(F32)
            masks.append([tags[lane : lane + 1, :] == tile_id for lane in range(LANES)])

        def rows(i, c):
            r0 = pl.multiple_of(i * 32, 32)
            start = t * (TILE * 4) + i * 128 + 2 * s
            acc = jnp.concatenate(
                [front[pl.ds(start, 32, stride=4), :], front[pl.ds(start + 1, 32, stride=4), :]], axis=1
            )
            for src in range(NX):
                for lane in range(LANES):
                    v = recv[src, pl.ds(lane * TILE + r0, 32), :].astype(F32)
                    acc = acc + jnp.where(masks[src][lane], v, 0.0)
            dst[pl.ds(r0, 32), :] = acc
            return c

        lax.fori_loop(0, TILE // 32, rows, 0)

    def part(i):
        row0, rows, width = CHUNKS[i]
        return w.at[row0 : row0 + rows, 0:width]

    def relay_factor():
        for i in range(NCHUNK):
            drain(part(i), w_r.at[i])

            def pass_on(*device):
                send(part(i), part(i), w_s, w_r.at[i], at(*device))

            @pl.when(is_helper)
            def _():
                for j in range(1, NX):
                    pass_on(j, 0, 0, 1)

            @pl.when((y == 0) & (z == 0) & (h == 1))
            def _():
                for j in range(1, NY):
                    pass_on(x, j, 0, 1)

            @pl.when((z == 0) & (h == 1))
            def _():
                for j in range(1, NZ):
                    pass_on(x, y, j, 1)

            @pl.when((h == 1) & jnp.logical_not(is_helper))
            def _():
                pass_on(x, y, z, 0)

    def spread_rows():
        def spread(p, c):
            view = pl.ds(pl.multiple_of(p * ZPIECE, ZPIECE), ZPIECE)
            send(brow.at[:, view, :], brow.at[:, view, :], rs_s, rs_r, at(x, y, p, 0))
            send(brow.at[:, 0:ZPIECE, :], brow.at[:, 0:ZPIECE, :], ra_s, ra_r.at[0], at(x, y, p, 0))
            return c

        lax.fori_loop(1, NZ, spread, 0)

    @pl.when(q == 0)
    def _():
        wait_children()
        assemble(0, 0, brow.at[0])

        @pl.when(k != 0)
        def _():
            def scatter(p, c):
                view = pl.ds(pl.multiple_of(p * PIECE, PIECE), PIECE)
                @pl.when((p != k) | (my_q != 0))
                def _():
                    send(brow.at[0, view, :], bcol.at[my_s, view, :], cs_s, cs_r.at[my_s],
                         at(p // NY, lax.rem(p, NY), my_z, my_h))
                return c

            lax.fori_loop(0, OWNERS, scatter, 0)

        @pl.when(k == NCOL)
        def _():
            bcol[1, NCOL * PIECE : (NCOL + 1) * PIECE, :] = brow[0, NCOL * PIECE : (NCOL + 1) * PIECE, :]

        for t in range(1, TR):
            assemble(t, 0, brow.at[t])

        send(brow, brow, rf_s, rf_r, at(x, y, 0, 1))

        @pl.when(k != 0)
        def _():
            spread_rows()

    @pl.when(is_root)
    def _():
        a = brow[0]
        m_ref[:, :TILE] = 0.5 * (a + a.T)
        ii = lax.broadcasted_iota(jnp.int32, (TILE, TILE), 0)
        jj = lax.broadcasted_iota(jnp.int32, (TILE, TILE), 1)
        m_ref[:, TILE:] = jnp.where(ii == jj, 1.0, 0.0)

        def step(b, c):
            cholesky_step(b, m_ref, u_ref, w)
            for i in range(NCHUNK):
                @pl.when(b == (CHUNKS[i][0] + CHUNKS[i][1]) // NB - 1)
                def _():
                    send(part(i), part(i), w_s, w_r.at[i], at(0, 0, 0, 1))
            return c

        lax.fori_loop(0, NBLOCK, step, 0)

    @pl.when(is_helper)
    def _():
        drain(brow, rf_r)
        spread_rows()

    @pl.when(q != 0)
    def _():
        drain(bcol.at[0, 0:PIECE, :], cs_r.at[0])

    @pl.when(jnp.logical_not((q == 0) & (k == NCOL)))
    def _():
        drain(bcol.at[0, 0:PIECE, :], cs_r.at[1])

    mine = pl.ds(pl.multiple_of(k * PIECE, PIECE), PIECE)

    def gather_columns(i, c):
        p = lax.rem(k + i, OWNERS)
        send(bcol.at[:, mine, :], bcol.at[:, mine, :], ca_s, ca_r, at(p // NY, lax.rem(p, NY), z, h))
        return c

    lax.fori_loop(1, OWNERS, gather_columns, 0)

    @pl.when((h == 0) & (z != 0))
    def _():
        drain(brow.at[:, 0:ZPIECE, :], rs_r)
        view = pl.ds(pl.multiple_of(z * ZPIECE, ZPIECE), ZPIECE)

        def gather_rows(i, c):
            to = lax.rem(z + i, NZ)
            @pl.when(to != 0)
            def _():
                send(brow.at[:, view, :], brow.at[:, view, :], ra_s, ra_r.at[z], at(x, y, to, 0))
            return c

        lax.fori_loop(1, NZ, gather_rows, 0)

    @pl.when((z == 0) & (h == 1))
    def _():
        relay_factor()

    @pl.when(q != 0)
    def _():
        wait_children()

        def all_rows(t, c):
            assemble(t, 0, asm.at[0, t])
            return c

        lax.fori_loop(0, TR, all_rows, 0)

    def second_rows(t, c):
        assemble(t, 1, asm.at[1, t])
        return c

    lax.fori_loop(0, TR, second_rows, 0)

    @pl.when((h == 0) & (z != 0))
    def _():
        def one(i, c):
            frm = lax.rem(z + i, NZ)
            drain(brow.at[:, 0:ZPIECE, :], ra_r.at[frm])
            return c

        lax.fori_loop(1, NZ, one, 0)
        send(brow, brow, rf_s, rf_r, at(x, y, z, 1))

    @pl.when(jnp.logical_not(((z == 0) & (h == 1)) | is_root))
    def _():
        relay_factor()

    drain(bcol.at[:, 0 : TILE - PIECE, :], ca_r)

    @pl.when((h == 1) & jnp.logical_not(is_helper))
    def _():
        drain(brow, rf_r)

    winv = w[...]
    pcol = [nt(bcol[s], winv) for s in range(2)]

    def update(t, c):
        panel = nt(brow[t], winv)
        first = (k == 0) & (t == 0)
        for s in range(2):
            tile = asm[s, t] - nt(panel, pcol[s])
            tile = jnp.where(first, 0.0, tile)
            if s == 0:
                tile = jnp.where(q == 0, panel, tile)
            start = t * (TILE * 4) + 2 * s
            out[pl.ds(start, TILE, stride=4), :] = tile[:, :128]
            out[pl.ds(start + 1, TILE, stride=4), :] = tile[:, 128:]
        return c

    lax.fori_loop(0, TR, update, 0)

    @pl.when(is_root)
    def _():
        ii = lax.broadcasted_iota(jnp.int32, (TILE, TILE), 0)
        jj = lax.broadcasted_iota(jnp.int32, (TILE, TILE), 1)
        factor = jnp.where(ii >= jj, u_ref[...].T, 0.0)
        out[pl.ds(0, TILE, stride=4), :] = factor[:, :128]
        out[pl.ds(1, TILE, stride=4), :] = factor[:, 128:]

    for i in range(1, NX):
        drain(stage.at[0], ch_s.at[i])

    def each(count, view, sem):
        def one(i, c):
            drain(view, sem)
            return c
        lax.fori_loop(0, count, one, 0)

    @pl.when((q == 0) & (k != 0))
    def _():
        each(jnp.where(k == NCOL, OWNERS - 1, OWNERS), brow.at[0, 0:PIECE, :], cs_s)

    each(OWNERS - 1, bcol.at[:, 0:PIECE, :], ca_s)

    @pl.when(((q == 0) & (k != 0)) | is_helper)
    def _():
        each(NZ - 1, brow.at[:, 0:ZPIECE, :], rs_s)
        each(NZ - 1, brow.at[:, 0:ZPIECE, :], ra_s)

    @pl.when((h == 0) & (z != 0))
    def _():
        each(NZ - 2, brow.at[:, 0:ZPIECE, :], ra_s)

    @pl.when(h == 0)
    def _():
        drain(brow, rf_s)

    sent = (
        jnp.where((h == 1) & (k == 0) & (z == 0), NX - 1, 0)
        + jnp.where((h == 1) & (y == 0) & (z == 0), NY - 1, 0)
        + jnp.where((h == 1) & (z == 0), NZ - 1, 0)
        + jnp.where((h == 1) & jnp.logical_not(is_helper), 1, 0)
        + jnp.where(is_root, 1, 0)
    )
    for i in range(NCHUNK):
        each(sent, part(i), w_s)


def local(front_tiles, child_tiles, target_rows, target_cols, live_counts):
    front = front_tiles.reshape(TR * TILE * 4, 128)
    child = child_tiles.reshape(SLOTS, TILE, TILE)
    hbm = pl.BlockSpec(memory_space=pltpu.HBM)
    dma = pltpu.SemaphoreType.DMA
    out = pl.pallas_call(
        kernel,
        out_shape=pltpu.VMEM(front.shape, F32),
        in_specs=[hbm] * 5,
        out_specs=pl.BlockSpec(memory_space=pltpu.VMEM),
        scratch_shapes=[
            pltpu.VMEM(front.shape, F32),
            pltpu.VMEM(child.shape, BF16),
            pltpu.SMEM((SLOTS,), jnp.int32),
            pltpu.SMEM((SLOTS,), jnp.int32),
            pltpu.SMEM((1,), jnp.int32),
            dma((5,)),
            pltpu.VMEM((NX, STAGE_ROWS, TILE), BF16),
            pltpu.VMEM((NX, STAGE_ROWS, TILE), BF16),
            pltpu.VMEM((2, TR, TILE, TILE), F32),
            pltpu.VMEM((TR, TILE, TILE), F32),
            pltpu.VMEM((2, TILE, TILE), F32),
            pltpu.VMEM((TILE, TILE), F32),
            pltpu.VMEM((TILE, 2 * TILE), F32),
            pltpu.VMEM((TILE, TILE), F32),
            dma((NX,)), dma((NX,)),
            dma, dma((2,)),
            dma, dma,
            dma, dma,
            dma, dma((NZ,)),
            dma, dma,
            dma, dma((NCHUNK,)),
        ],
        compiler_params=pltpu.CompilerParams(
            collective_id=0, has_side_effects=True, vmem_limit_bytes=56 * 1024 * 1024
        ),
        cost_estimate=pl.CostEstimate(flops=11 * 2 * TILE**3, bytes_accessed=4 * 1024 * 1024, transcendentals=0),
        name="front_panel",
    )(front, child, target_rows.reshape(SLOTS), target_cols.reshape(SLOTS), live_counts.reshape(1))
    return out.reshape(front_tiles.shape)


def solution(mesh):
    placed = (
        P(None, ("cube", "row"), None, None, "col", None),
        P("cube", "row", "col", None, None, None),
        P("cube", "row", "col", None),
        P("cube", "row", "col", None),
        P("cube", "row", "col"),
    )
    return jax.shard_map(
        local,
        mesh=mesh,
        in_specs=placed,
        out_specs=P(None, ("cube", "row"), None, None, "col", None),
        check_vma=False,
    )
```

```python
import jax
import jax.numpy as jnp
from jax import lax
from jax.experimental import pallas as pl
from jax.experimental.pallas import tpu as pltpu
from jax.sharding import PartitionSpec as P

MESH = pl.DeviceIdType.MESH
HIGHEST = lax.Precision.HIGHEST
F32 = jnp.float32
BF16 = jnp.bfloat16

NX, NY, NZ = 4, 8, 8
OWNERS = NX * NY
NCOL = 2 * NZ
TILE = 256
TR = 3
SLOTS = 4
LANES = 2
META = LANES * TILE
STAGE_ROWS = META + 16
PIECE = TILE // OWNERS
GROUP = PIECE * NY
ZPIECE = TILE // NZ
NB = 32
NBLOCK = TILE // NB
CHUNKS = ((0, 128, 128), (128, 64, 256), (192, 32, 256), (224, 32, 256))
NCHUNK = len(CHUNKS)


def nt(a, b):
    return lax.dot_general(a, b, (((1,), (1,)), ((), ())), precision=lax.Precision.HIGH, preferred_element_type=F32)


def drain(view, sem, times=1):
    for _ in range(times):
        pltpu.make_async_copy(view, view, sem).wait()


def cholesky_step(b, m_ref, u_ref, w_ref):
    row0 = pl.multiple_of(b * NB, NB)
    block = m_ref[pl.ds(row0, NB), :]
    half = jnp.where(b < NBLOCK // 2, block[:, :128], block[:, 128:256])
    diag = pltpu.roll(half, lax.rem(128 - lax.rem(b * NB, 128), 128), 1)
    parts = [block[:, 128 * i : 128 * (i + 1)] for i in range(4)] + [diag]
    rows = lax.broadcasted_iota(jnp.int32, (NB, 128), 0)
    for g in range(NB // 8):
        base = 8 * g
        cols = [jnp.broadcast_to(parts[4][base:, base + j : base + j + 1], (NB - base, 128)) for j in range(8)]
        live = [p[base:] for p in parts]
        below = rows[base:] - base
        for kk in range(8):
            pivot = cols[kk][kk : kk + 1, :]
            inv = lax.rsqrt(pivot)
            inv = inv * (1.5 - 0.5 * pivot * inv * inv)
            col = cols[kk] * inv
            masked = jnp.where(below > kk, col, 0.0)
            for j in range(kk + 1, 8):
                cols[j] = cols[j] - masked * col[j : j + 1, :]
            for i in range(5):
                top = live[i][kk : kk + 1, :] * inv
                live[i] = jnp.where(below == kk, top, live[i] - masked * top)
        parts = [l if g == 0 else jnp.concatenate([p[:base], l], axis=0) for p, l in zip(parts, live)]
    u = jnp.concatenate(parts[:2], axis=1)
    winv = jnp.concatenate(parts[2:4], axis=1)
    u_ref[pl.ds(row0, NB), :] = u
    w_ref[pl.ds(row0, NB), :] = winv
    both = jnp.concatenate(parts[:4], axis=1)
    b1 = both.astype(BF16)
    rest = both - b1.astype(F32)
    b2 = rest.astype(BF16)
    b3 = (rest - b2.astype(F32)).astype(BF16)
    a1, a2, a3 = b1[:, :TILE], b2[:, :TILE], b3[:, :TILE]
    lhs = jnp.concatenate([a1, a1, a2, a2, a1, a3], axis=0)
    rhs = jnp.concatenate([b1, b2, b1, b2, b3, b1], axis=0)
    m_ref[...] -= lax.dot_general(lhs, rhs, (((0,), (0,)), ((), ())), preferred_element_type=F32)


def kernel(
    front_h, child_h, trow_h, tcol_h, live_h, out,
    front, child, trow, tcol, live, in_s, stage, recv, asm, brow, bcol, w, m_ref, u_ref,
    ch_s, ch_r, cs_s, cs_r, cy_s, cy_r, cx_s, cx_r, rs_s, rs_r, ra_s, ra_r, rf_s, rf_r, w_s, w_r, go,
):
    x, y, q = lax.axis_index("cube"), lax.axis_index("row"), lax.axis_index("col")
    z, h = q // 2, q % 2
    k = x * NY + y
    is_root = (k == 0) & (q == 0)
    is_helper = (k == 0) & (q == 1)

    loads = [
        pltpu.make_async_copy(src, dst, in_s.at[i])
        for i, (src, dst) in enumerate(
            [(trow_h, trow), (tcol_h, tcol), (live_h, live), (child_h, child), (front_h, front)]
        )
    ]
    for load in loads:
        load.start()

    def at(xx, yy, zz, hh):
        return (xx, yy, zz * 2 + hh)

    def send(src, dst, ssem, rsem, device):
        pltpu.make_async_remote_copy(
            src_ref=src, dst_ref=dst, send_sem=ssem, recv_sem=rsem, device_id=device, device_id_type=MESH
        ).start()

    my_s, my_q = k // NCOL, k % NCOL
    my_z, my_h = my_q // 2, my_q % 2

    barrier = pltpu.get_barrier_semaphore()

    def greet(device):
        pl.semaphore_signal(barrier, inc=1, device_id=device, device_id_type=MESH)

    def greet_plane(i, c):
        p = lax.rem(k + i, OWNERS)
        greet(at(p // NY, lax.rem(p, NY), z, h))
        return c

    def greet_z(i, c):
        greet(at(x, y, lax.rem(z + i, NZ), h))
        return c

    lax.fori_loop(1, NX * NY, greet_plane, 0)
    lax.fori_loop(1, NZ, greet_z, 0)
    greet(at(x, y, z, 1 - h))

    @pl.when((q == 0) & (my_h == 1) & (my_z != 0))
    def _():
        greet(at(x, y, my_z, my_h))

    speaks = (my_q == q) & (q != 0)

    for load in loads[:4]:
        load.wait()
    alive = [jnp.where(m < live[0], 1, 0) for m in range(SLOTS)]
    cube_of = [lax.rem(trow[m], OWNERS) // NY for m in range(SLOTS)]
    tile_of = [(trow[m] // OWNERS) * 2 + tcol[m] // NCOL for m in range(SLOTS)]
    meta_row = lax.broadcasted_iota(jnp.int32, (16, TILE), 0)
    for d in range(NX):
        seen = 0
        index = [0, 0]
        label = [-1, -1]
        for m in range(SLOTS):
            hit = alive[m] * jnp.where(cube_of[m] == d, 1, 0)
            for lane in range(LANES):
                here = hit * jnp.where(seen == lane, 1, 0)
                index[lane] = index[lane] + here * m
                label[lane] = label[lane] + here * (tile_of[m] + 1)
            seen = seen + hit
        for lane in range(LANES):
            stage[d, lane * TILE : (lane + 1) * TILE, :] = child[index[lane]]
        tags = jnp.where(meta_row == 0, label[0], jnp.where(meta_row == 1, label[1], -1))
        stage[d, META:, :] = tags.astype(F32).astype(BF16)

    w[: TILE // 2, TILE // 2 :] = jnp.zeros((TILE // 2, TILE // 2), F32)

    loads[4].wait()
    pl.semaphore_wait(barrier, NX * NY - 1 + NZ - 1 + 1 + jnp.where(speaks & (h == 1) & (z != 0), 1, 0))

    @pl.when(speaks)
    def _():
        pl.semaphore_signal(go, inc=1, device_id=at(x, y, 0, 0), device_id_type=MESH)

    for i in range(1, NX):
        d = lax.rem(x + i, NX)
        send(stage.at[d], recv.at[x], ch_s.at[i], ch_r.at[x], at(d, y, z, h))
    recv[x] = stage[x]

    def wait_children():
        for i in range(1, NX):
            src = lax.rem(x + i, NX)
            drain(recv.at[src], ch_r.at[src])

    def assemble(t, s, dst):
        tile_id = (t * 2 + s).astype(F32) if hasattr(t, "astype") else float(t * 2 + s)
        masks = []
        for src in range(NX):
            tags = recv[src, META:, :].astype(F32)
            masks.append([tags[lane : lane + 1, :] == tile_id for lane in range(LANES)])

        def rows(i, c):
            r0 = pl.multiple_of(i * 32, 32)
            start = t * (TILE * 4) + i * 128 + 2 * s
            acc = jnp.concatenate(
                [front[pl.ds(start, 32, stride=4), :], front[pl.ds(start + 1, 32, stride=4), :]], axis=1
            )
            for src in range(NX):
                for lane in range(LANES):
                    v = recv[src, pl.ds(lane * TILE + r0, 32), :].astype(F32)
                    acc = acc + jnp.where(masks[src][lane], v, 0.0)
            dst[pl.ds(r0, 32), :] = acc
            return c

        lax.fori_loop(0, TILE // 32, rows, 0)

    def part(i):
        row0, rows, width = CHUNKS[i]
        return w.at[row0 : row0 + rows, 0:width]

    def relay_factor(first, last):
        for i in range(first, last):
            drain(part(i), w_r.at[i])

            def pass_on(*device):
                send(part(i), part(i), w_s, w_r.at[i], at(*device))

            @pl.when(is_helper)
            def _():
                for j in range(1, NX):
                    pass_on(j, 0, 0, 1)

            @pl.when((y == 0) & (z == 0) & (h == 1))
            def _():
                for j in range(1, NY):
                    pass_on(x, j, 0, 1)

            @pl.when((z == 0) & (h == 1))
            def _():
                for j in range(1, NZ):
                    pass_on(x, y, j, 1)

            @pl.when((h == 1) & jnp.logical_not(is_helper))
            def _():
                pass_on(x, y, z, 0)

    def spread_rows():
        def spread(p, c):
            view = pl.ds(pl.multiple_of(p * ZPIECE, ZPIECE), ZPIECE)
            send(brow.at[:, view, :], brow.at[:, view, :], rs_s, rs_r, at(x, y, p, 0))
            send(brow.at[:, 0:ZPIECE, :], brow.at[:, 0:ZPIECE, :], ra_s, ra_r.at[0], at(x, y, p, 0))
            return c

        lax.fori_loop(1, NZ, spread, 0)

    @pl.when(q == 0)
    def _():
        wait_children()
        assemble(0, 0, brow.at[0])

        @pl.when(my_q != 0)
        def _():
            pl.semaphore_wait(go, 1)

        @pl.when(k != 0)
        def _():
            def scatter(p, c):
                view = pl.ds(pl.multiple_of(p * PIECE, PIECE), PIECE)
                @pl.when((p != k) | (my_q != 0))
                def _():
                    send(brow.at[0, view, :], bcol.at[my_s, view, :], cs_s, cs_r.at[my_s],
                         at(p // NY, lax.rem(p, NY), my_z, my_h))
                return c

            lax.fori_loop(0, OWNERS, scatter, 0)

        @pl.when(k == NCOL)
        def _():
            bcol[1, NCOL * PIECE : (NCOL + 1) * PIECE, :] = brow[0, NCOL * PIECE : (NCOL + 1) * PIECE, :]

        for t in range(1, TR):
            assemble(t, 0, brow.at[t])

        send(brow, brow, rf_s, rf_r, at(x, y, 0, 1))

        @pl.when(k != 0)
        def _():
            spread_rows()

    @pl.when(is_root)
    def _():
        a = brow[0]
        m_ref[:, :TILE] = 0.5 * (a + a.T)
        ii = lax.broadcasted_iota(jnp.int32, (TILE, TILE), 0)
        jj = lax.broadcasted_iota(jnp.int32, (TILE, TILE), 1)
        m_ref[:, TILE:] = jnp.where(ii == jj, 1.0, 0.0)

        def step(b, c):
            cholesky_step(b, m_ref, u_ref, w)
            for i in range(NCHUNK):
                @pl.when(b == (CHUNKS[i][0] + CHUNKS[i][1]) // NB - 1)
                def _():
                    send(part(i), part(i), w_s, w_r.at[i], at(0, 0, 0, 1))
            return c

        lax.fori_loop(0, NBLOCK, step, 0)

    @pl.when(is_helper)
    def _():
        drain(brow, rf_r)
        spread_rows()

    @pl.when(q != 0)
    def _():
        drain(bcol.at[0, 0:PIECE, :], cs_r.at[0])

    @pl.when(jnp.logical_not((q == 0) & (k == NCOL)))
    def _():
        drain(bcol.at[0, 0:PIECE, :], cs_r.at[1])

    mine = pl.ds(pl.multiple_of(k * PIECE, PIECE), PIECE)
    for i in range(1, NY):
        send(bcol.at[:, mine, :], bcol.at[:, mine, :], cy_s, cy_r, at(x, lax.rem(y + i, NY), z, h))

    def group(i):
        return bcol.at[:, pl.ds(pl.multiple_of(i * GROUP, GROUP), GROUP), :]

    def gather_columns():
        drain(bcol.at[:, 0 : GROUP - PIECE, :], cy_r)
        for i in range(1, NX):
            send(group(x), group(x), cx_s, cx_r.at[x], at(lax.rem(x + i, NX), y, z, h))

    early = (y == 0) & (z == 0) & (h == 1)
    middle = (y != 0) & (z == 0) & (h == 1)

    @pl.when((h == 0) & (z != 0))
    def _():
        drain(brow.at[:, 0:ZPIECE, :], rs_r)
        view = pl.ds(pl.multiple_of(z * ZPIECE, ZPIECE), ZPIECE)

        def gather_rows(i, c):
            to = lax.rem(z + i, NZ)
            @pl.when(to != 0)
            def _():
                send(brow.at[:, view, :], brow.at[:, view, :], ra_s, ra_r.at[z], at(x, y, to, 0))
            return c

        lax.fori_loop(1, NZ, gather_rows, 0)

    @pl.when(early)
    def _():
        relay_factor(0, NCHUNK)
        gather_columns()

    @pl.when(middle)
    def _():
        relay_factor(0, 1)
        gather_columns()
        relay_factor(1, NCHUNK)

    @pl.when((z != 0) | (h == 0))
    def _():
        gather_columns()

    @pl.when(q != 0)
    def _():
        wait_children()

        def all_rows(t, c):
            assemble(t, 0, asm.at[0, t])
            return c

        lax.fori_loop(0, TR, all_rows, 0)

    def second_rows(t, c):
        assemble(t, 1, asm.at[1, t])
        return c

    lax.fori_loop(0, TR, second_rows, 0)

    @pl.when((h == 0) & (z != 0))
    def _():
        def one(i, c):
            frm = lax.rem(z + i, NZ)
            drain(brow.at[:, 0:ZPIECE, :], ra_r.at[frm])
            return c

        lax.fori_loop(1, NZ, one, 0)
        send(brow, brow, rf_s, rf_r, at(x, y, z, 1))

    @pl.when(jnp.logical_not(((z == 0) & (h == 1)) | is_root))
    def _():
        relay_factor(0, NCHUNK)

    for i in range(1, NX):
        frm = lax.rem(x + i, NX)
        drain(group(frm), cx_r.at[frm])

    @pl.when((h == 1) & jnp.logical_not(is_helper))
    def _():
        drain(brow, rf_r)

    winv = w[...]
    pcol = [nt(bcol[s], winv) for s in range(2)]

    def update(t, c):
        panel = nt(brow[t], winv)
        first = (k == 0) & (t == 0)
        for s in range(2):
            tile = asm[s, t] - nt(panel, pcol[s])
            tile = jnp.where(first, 0.0, tile)
            if s == 0:
                tile = jnp.where(q == 0, panel, tile)
            start = t * (TILE * 4) + 2 * s
            out[pl.ds(start, TILE, stride=4), :] = tile[:, :128]
            out[pl.ds(start + 1, TILE, stride=4), :] = tile[:, 128:]
        return c

    lax.fori_loop(0, TR, update, 0)

    @pl.when(is_root)
    def _():
        ii = lax.broadcasted_iota(jnp.int32, (TILE, TILE), 0)
        jj = lax.broadcasted_iota(jnp.int32, (TILE, TILE), 1)
        factor = jnp.where(ii >= jj, u_ref[...].T, 0.0)
        out[pl.ds(0, TILE, stride=4), :] = factor[:, :128]
        out[pl.ds(1, TILE, stride=4), :] = factor[:, 128:]

    for i in range(1, NX):
        drain(stage.at[0], ch_s.at[i])

    def each(count, view, sem):
        def one(i, c):
            drain(view, sem)
            return c
        lax.fori_loop(0, count, one, 0)

    @pl.when((q == 0) & (k != 0))
    def _():
        each(jnp.where(k == NCOL, OWNERS - 1, OWNERS), brow.at[0, 0:PIECE, :], cs_s)

    each(NY - 1, bcol.at[:, 0:PIECE, :], cy_s)
    each(NX - 1, bcol.at[:, 0:GROUP, :], cx_s)

    @pl.when(((q == 0) & (k != 0)) | is_helper)
    def _():
        each(NZ - 1, brow.at[:, 0:ZPIECE, :], rs_s)
        each(NZ - 1, brow.at[:, 0:ZPIECE, :], ra_s)

    @pl.when((h == 0) & (z != 0))
    def _():
        each(NZ - 2, brow.at[:, 0:ZPIECE, :], ra_s)

    @pl.when(h == 0)
    def _():
        drain(brow, rf_s)

    sent = (
        jnp.where((h == 1) & (k == 0) & (z == 0), NX - 1, 0)
        + jnp.where((h == 1) & (y == 0) & (z == 0), NY - 1, 0)
        + jnp.where((h == 1) & (z == 0), NZ - 1, 0)
        + jnp.where((h == 1) & jnp.logical_not(is_helper), 1, 0)
        + jnp.where(is_root, 1, 0)
    )
    for i in range(NCHUNK):
        each(sent, part(i), w_s)


def local(front_tiles, child_tiles, target_rows, target_cols, live_counts):
    front = front_tiles.reshape(TR * TILE * 4, 128)
    child = child_tiles.reshape(SLOTS, TILE, TILE)
    hbm = pl.BlockSpec(memory_space=pltpu.HBM)
    dma = pltpu.SemaphoreType.DMA
    out = pl.pallas_call(
        kernel,
        out_shape=pltpu.VMEM(front.shape, F32),
        in_specs=[hbm] * 5,
        out_specs=pl.BlockSpec(memory_space=pltpu.VMEM),
        scratch_shapes=[
            pltpu.VMEM(front.shape, F32),
            pltpu.VMEM(child.shape, BF16),
            pltpu.SMEM((SLOTS,), jnp.int32),
            pltpu.SMEM((SLOTS,), jnp.int32),
            pltpu.SMEM((1,), jnp.int32),
            dma((5,)),
            pltpu.VMEM((NX, STAGE_ROWS, TILE), BF16),
            pltpu.VMEM((NX, STAGE_ROWS, TILE), BF16),
            pltpu.VMEM((2, TR, TILE, TILE), F32),
            pltpu.VMEM((TR, TILE, TILE), F32),
            pltpu.VMEM((2, TILE, TILE), F32),
            pltpu.VMEM((TILE, TILE), F32),
            pltpu.VMEM((TILE, 2 * TILE), F32),
            pltpu.VMEM((TILE, TILE), F32),
            dma((NX,)), dma((NX,)),
            dma, dma((2,)),
            dma, dma,
            dma, dma((NX,)),
            dma, dma,
            dma, dma((NZ,)),
            dma, dma,
            dma, dma((NCHUNK,)),
            pltpu.SemaphoreType.REGULAR,
        ],
        compiler_params=pltpu.CompilerParams(
            collective_id=0, has_side_effects=True, vmem_limit_bytes=56 * 1024 * 1024
        ),
        cost_estimate=pl.CostEstimate(flops=11 * 2 * TILE**3, bytes_accessed=4 * 1024 * 1024, transcendentals=0),
        name="front_panel",
    )(front, child, target_rows.reshape(SLOTS), target_cols.reshape(SLOTS), live_counts.reshape(1))
    return out.reshape(front_tiles.shape)


def solution(mesh):
    placed = (
        P(None, ("cube", "row"), None, None, "col", None),
        P("cube", "row", "col", None, None, None),
        P("cube", "row", "col", None),
        P("cube", "row", "col", None),
        P("cube", "row", "col"),
    )
    return jax.shard_map(
        local,
        mesh=mesh,
        in_specs=placed,
        out_specs=P(None, ("cube", "row"), None, None, "col", None),
        check_vma=False,
    )
```

```python
import jax
import jax.numpy as jnp
from jax import lax
from jax.experimental import pallas as pl
from jax.experimental.pallas import tpu as pltpu
from jax.sharding import PartitionSpec as P

MESH = pl.DeviceIdType.MESH
HIGHEST = lax.Precision.HIGHEST
F32 = jnp.float32
BF16 = jnp.bfloat16

NX, NY, NZ = 4, 8, 8
OWNERS = NX * NY
NCOL = 2 * NZ
TILE = 256
TR = 3
SLOTS = 4
LANES = 2
META = LANES * TILE
STAGE_ROWS = META + 16
PIECE = TILE // OWNERS
GROUP = PIECE * NY
ZPIECE = TILE // NZ
CODED_ROWS = TR * ZPIECE + 16
LIMIT, STEPS = 80.0, 32767.0
NB = 32
NBLOCK = TILE // NB
CHUNKS = ((0, 128, 128), (128, 64, 256), (192, 32, 256), (224, 32, 256))
NCHUNK = len(CHUNKS)


def nt(a, b):
    return lax.dot_general(a, b, (((1,), (1,)), ((), ())), precision=lax.Precision.HIGH, preferred_element_type=F32)


def drain(view, sem, times=1):
    for _ in range(times):
        pltpu.make_async_copy(view, view, sem).wait()


def cholesky_step(b, m_ref, u_ref, w_ref):
    row0 = pl.multiple_of(b * NB, NB)
    block = m_ref[pl.ds(row0, NB), :]
    half = jnp.where(b < NBLOCK // 2, block[:, :128], block[:, 128:256])
    diag = pltpu.roll(half, lax.rem(128 - lax.rem(b * NB, 128), 128), 1)
    parts = [block[:, 128 * i : 128 * (i + 1)] for i in range(4)] + [diag]
    rows = lax.broadcasted_iota(jnp.int32, (NB, 128), 0)
    for g in range(NB // 8):
        base = 8 * g
        cols = [jnp.broadcast_to(parts[4][base:, base + j : base + j + 1], (NB - base, 128)) for j in range(8)]
        live = [p[base:] for p in parts]
        below = rows[base:] - base
        for kk in range(8):
            pivot = cols[kk][kk : kk + 1, :]
            inv = lax.rsqrt(pivot)
            inv = inv * (1.5 - 0.5 * pivot * inv * inv)
            col = cols[kk] * inv
            masked = jnp.where(below > kk, col, 0.0)
            for j in range(kk + 1, 8):
                cols[j] = cols[j] - masked * col[j : j + 1, :]
            for i in range(5):
                top = live[i][kk : kk + 1, :] * inv
                live[i] = jnp.where(below == kk, top, live[i] - masked * top)
        parts = [l if g == 0 else jnp.concatenate([p[:base], l], axis=0) for p, l in zip(parts, live)]
    u = jnp.concatenate(parts[:2], axis=1)
    winv = jnp.concatenate(parts[2:4], axis=1)
    u_ref[pl.ds(row0, NB), :] = u
    w_ref[pl.ds(row0, NB), :] = winv
    both = jnp.concatenate(parts[:4], axis=1)
    b1 = both.astype(BF16)
    rest = both - b1.astype(F32)
    b2 = rest.astype(BF16)
    b3 = (rest - b2.astype(F32)).astype(BF16)
    a1, a2, a3 = b1[:, :TILE], b2[:, :TILE], b3[:, :TILE]
    lhs = jnp.concatenate([a1, a1, a2, a2, a1, a3], axis=0)
    rhs = jnp.concatenate([b1, b2, b1, b2, b3, b1], axis=0)
    m_ref[...] -= lax.dot_general(lhs, rhs, (((0,), (0,)), ((), ())), preferred_element_type=F32)


def kernel(
    front_h, child_h, trow_h, tcol_h, live_h, out,
    front, child, trow, tcol, live, in_s, stage, recv, asm, brow, coded, bcol, w, m_ref, u_ref,
    ch_s, ch_r, cs_s, cs_r, cy_s, cy_r, cx_s, cx_r, rs_s, rs_r, ra_s, ra_r, rf_s, rf_r, w_s, w_r, go,
):
    x, y, q = lax.axis_index("cube"), lax.axis_index("row"), lax.axis_index("col")
    z, h = q // 2, q % 2
    k = x * NY + y
    is_root = (k == 0) & (q == 0)
    is_helper = (k == 0) & (q == 1)

    loads = [
        pltpu.make_async_copy(src, dst, in_s.at[i])
        for i, (src, dst) in enumerate(
            [(trow_h, trow), (tcol_h, tcol), (live_h, live), (child_h, child), (front_h, front)]
        )
    ]
    for load in loads:
        load.start()

    def at(xx, yy, zz, hh):
        return (xx, yy, zz * 2 + hh)

    def send(src, dst, ssem, rsem, device):
        pltpu.make_async_remote_copy(
            src_ref=src, dst_ref=dst, send_sem=ssem, recv_sem=rsem, device_id=device, device_id_type=MESH
        ).start()

    my_s, my_q = k // NCOL, k % NCOL
    my_z, my_h = my_q // 2, my_q % 2

    barrier = pltpu.get_barrier_semaphore()

    def greet(device):
        pl.semaphore_signal(barrier, inc=1, device_id=device, device_id_type=MESH)

    def greet_plane(i, c):
        p = lax.rem(k + i, OWNERS)
        greet(at(p // NY, lax.rem(p, NY), z, h))
        return c

    def greet_z(i, c):
        greet(at(x, y, lax.rem(z + i, NZ), h))
        return c

    lax.fori_loop(1, NX * NY, greet_plane, 0)
    lax.fori_loop(1, NZ, greet_z, 0)
    greet(at(x, y, z, 1 - h))

    @pl.when((q == 0) & (my_h == 1) & (my_z != 0))
    def _():
        greet(at(x, y, my_z, my_h))

    speaks = (my_q == q) & (q != 0)

    for load in loads[:4]:
        load.wait()
    alive = [jnp.where(m < live[0], 1, 0) for m in range(SLOTS)]
    cube_of = [lax.rem(trow[m], OWNERS) // NY for m in range(SLOTS)]
    tile_of = [(trow[m] // OWNERS) * 2 + tcol[m] // NCOL for m in range(SLOTS)]
    meta_row = lax.broadcasted_iota(jnp.int32, (16, TILE), 0)
    for d in range(NX):
        seen = 0
        index = [0, 0]
        label = [-1, -1]
        for m in range(SLOTS):
            hit = alive[m] * jnp.where(cube_of[m] == d, 1, 0)
            for lane in range(LANES):
                here = hit * jnp.where(seen == lane, 1, 0)
                index[lane] = index[lane] + here * m
                label[lane] = label[lane] + here * (tile_of[m] + 1)
            seen = seen + hit
        for lane in range(LANES):
            stage[d, lane * TILE : (lane + 1) * TILE, :] = child[index[lane]]
        tags = jnp.where(meta_row == 0, label[0], jnp.where(meta_row == 1, label[1], -1))
        stage[d, META:, :] = tags.astype(F32).astype(BF16)

    w[: TILE // 2, TILE // 2 :] = jnp.zeros((TILE // 2, TILE // 2), F32)

    loads[4].wait()
    pl.semaphore_wait(barrier, NX * NY - 1 + NZ - 1 + 1 + jnp.where(speaks & (h == 1) & (z != 0), 1, 0))

    @pl.when(speaks)
    def _():
        pl.semaphore_signal(go, inc=1, device_id=at(x, y, 0, 0), device_id_type=MESH)

    for i in range(1, NX):
        d = lax.rem(x + i, NX)
        send(stage.at[d], recv.at[x], ch_s.at[i], ch_r.at[x], at(d, y, z, h))
    recv[x] = stage[x]

    def wait_children():
        for i in range(1, NX):
            src = lax.rem(x + i, NX)
            drain(recv.at[src], ch_r.at[src])

    def assemble(t, s, dst):
        tile_id = (t * 2 + s).astype(F32) if hasattr(t, "astype") else float(t * 2 + s)
        masks = []
        for src in range(NX):
            tags = recv[src, META:, :].astype(F32)
            masks.append([tags[lane : lane + 1, :] == tile_id for lane in range(LANES)])

        def rows(i, c):
            r0 = pl.multiple_of(i * 32, 32)
            start = t * (TILE * 4) + i * 128 + 2 * s
            acc = jnp.concatenate(
                [front[pl.ds(start, 32, stride=4), :], front[pl.ds(start + 1, 32, stride=4), :]], axis=1
            )
            for src in range(NX):
                for lane in range(LANES):
                    v = recv[src, pl.ds(lane * TILE + r0, 32), :].astype(F32)
                    acc = acc + jnp.where(masks[src][lane], v, 0.0)
            dst[pl.ds(r0, 32), :] = acc
            return c

        lax.fori_loop(0, TILE // 32, rows, 0)

    def part(i):
        row0, rows, width = CHUNKS[i]
        return w.at[row0 : row0 + rows, 0:width]

    def relay_factor(first, last):
        for i in range(first, last):
            drain(part(i), w_r.at[i])

            def pass_on(*device):
                send(part(i), part(i), w_s, w_r.at[i], at(*device))

            @pl.when(is_helper)
            def _():
                for j in range(1, NX):
                    pass_on(j, 0, 0, 1)

            @pl.when((y == 0) & (z == 0) & (h == 1))
            def _():
                for j in range(1, NY):
                    pass_on(x, j, 0, 1)

            @pl.when((z == 0) & (h == 1))
            def _():
                for j in range(1, NZ):
                    pass_on(x, y, j, 1)

            @pl.when((h == 1) & jnp.logical_not(is_helper))
            def _():
                pass_on(x, y, z, 0)

    def encode(v):
        return ((v + (STEPS + 1.5)).astype(jnp.int32) - int(STEPS + 1)).astype(jnp.int16)

    def encode_rows():
        tag_row = lax.broadcasted_iota(jnp.int32, (16, TILE), 0)
        tags = jnp.zeros((16, TILE), F32)
        inverse = []
        for t in range(TR):
            peak = jnp.max(jnp.max(jnp.abs(brow[t]), axis=0, keepdims=True), axis=1, keepdims=True)
            level = jnp.floor(peak * (STEPS / LIMIT)) + 1.0
            level = jnp.broadcast_to(level, (1, TILE))
            tags = jnp.where(tag_row == t, level, tags)
            inverse.append((STEPS * STEPS / LIMIT) / level)

        def one(p, c):
            view = pl.ds(pl.multiple_of(p * ZPIECE, ZPIECE), ZPIECE)
            for t in range(TR):
                coded[p, t * ZPIECE : (t + 1) * ZPIECE, :] = encode(brow[t, view, :] * inverse[t])
            coded[p, TR * ZPIECE :, :] = tags.astype(jnp.int32).astype(jnp.int16)
            return c

        lax.fori_loop(0, NZ, one, 0)

    def decode_rows():
        def one(p, c):
            view = pl.ds(pl.multiple_of(p * ZPIECE, ZPIECE), ZPIECE)
            tags = coded[p, TR * ZPIECE :, :].astype(jnp.int32).astype(F32) * (LIMIT / (STEPS * STEPS))
            for t in range(TR):
                v = coded[p, t * ZPIECE : (t + 1) * ZPIECE, :].astype(jnp.int32).astype(F32)
                brow[t, view, :] = v * tags[t : t + 1, :]
            return c

        lax.fori_loop(0, NZ, one, 0)

    def spread_rows():
        encode_rows()

        def spread(p, c):
            send(coded.at[p], coded.at[p], rs_s, rs_r, at(x, y, p, 0))
            send(coded.at[0], coded.at[0], ra_s, ra_r.at[0], at(x, y, p, 0))
            return c

        lax.fori_loop(1, NZ, spread, 0)

    @pl.when(q == 0)
    def _():
        wait_children()
        assemble(0, 0, brow.at[0])

        @pl.when(my_q != 0)
        def _():
            pl.semaphore_wait(go, 1)

        @pl.when(k != 0)
        def _():
            def scatter(p, c):
                view = pl.ds(pl.multiple_of(p * PIECE, PIECE), PIECE)
                @pl.when((p != k) | (my_q != 0))
                def _():
                    send(brow.at[0, view, :], bcol.at[my_s, view, :], cs_s, cs_r.at[my_s],
                         at(p // NY, lax.rem(p, NY), my_z, my_h))
                return c

            lax.fori_loop(0, OWNERS, scatter, 0)

        @pl.when(k == NCOL)
        def _():
            bcol[1, NCOL * PIECE : (NCOL + 1) * PIECE, :] = brow[0, NCOL * PIECE : (NCOL + 1) * PIECE, :]

        for t in range(1, TR):
            assemble(t, 0, brow.at[t])

        send(brow, brow, rf_s, rf_r, at(x, y, 0, 1))

        @pl.when(k != 0)
        def _():
            spread_rows()

    @pl.when(is_root)
    def _():
        a = brow[0]
        m_ref[:, :TILE] = 0.5 * (a + a.T)
        ii = lax.broadcasted_iota(jnp.int32, (TILE, TILE), 0)
        jj = lax.broadcasted_iota(jnp.int32, (TILE, TILE), 1)
        m_ref[:, TILE:] = jnp.where(ii == jj, 1.0, 0.0)

        def step(b, c):
            cholesky_step(b, m_ref, u_ref, w)
            for i in range(NCHUNK):
                @pl.when(b == (CHUNKS[i][0] + CHUNKS[i][1]) // NB - 1)
                def _():
                    send(part(i), part(i), w_s, w_r.at[i], at(0, 0, 0, 1))
            return c

        lax.fori_loop(0, NBLOCK, step, 0)

    @pl.when(is_helper)
    def _():
        drain(brow, rf_r)
        spread_rows()

    @pl.when(q != 0)
    def _():
        drain(bcol.at[0, 0:PIECE, :], cs_r.at[0])

    @pl.when(jnp.logical_not((q == 0) & (k == NCOL)))
    def _():
        drain(bcol.at[0, 0:PIECE, :], cs_r.at[1])

    mine = pl.ds(pl.multiple_of(k * PIECE, PIECE), PIECE)
    for i in range(1, NY):
        send(bcol.at[:, mine, :], bcol.at[:, mine, :], cy_s, cy_r, at(x, lax.rem(y + i, NY), z, h))

    def group(i):
        return bcol.at[:, pl.ds(pl.multiple_of(i * GROUP, GROUP), GROUP), :]

    def gather_columns():
        drain(bcol.at[:, 0 : GROUP - PIECE, :], cy_r)
        for i in range(1, NX):
            send(group(x), group(x), cx_s, cx_r.at[x], at(lax.rem(x + i, NX), y, z, h))

    early = (y == 0) & (z == 0) & (h == 1)
    middle = (y != 0) & (z == 0) & (h == 1)

    @pl.when((h == 0) & (z != 0))
    def _():
        drain(coded.at[0], rs_r)

        def gather_rows(i, c):
            to = lax.rem(z + i, NZ)
            @pl.when(to != 0)
            def _():
                send(coded.at[z], coded.at[z], ra_s, ra_r.at[z], at(x, y, to, 0))
            return c

        lax.fori_loop(1, NZ, gather_rows, 0)

    @pl.when(early)
    def _():
        relay_factor(0, NCHUNK)
        gather_columns()

    @pl.when(middle)
    def _():
        relay_factor(0, 1)
        gather_columns()
        relay_factor(1, NCHUNK)

    @pl.when((z != 0) | (h == 0))
    def _():
        gather_columns()

    @pl.when(q != 0)
    def _():
        wait_children()

        def all_rows(t, c):
            assemble(t, 0, asm.at[0, t])
            return c

        lax.fori_loop(0, TR, all_rows, 0)

    def second_rows(t, c):
        assemble(t, 1, asm.at[1, t])
        return c

    lax.fori_loop(0, TR, second_rows, 0)

    @pl.when((h == 0) & (z != 0))
    def _():
        def one(i, c):
            frm = lax.rem(z + i, NZ)
            drain(coded.at[0], ra_r.at[frm])
            return c

        lax.fori_loop(1, NZ, one, 0)
        send(coded, coded, rf_s, rf_r, at(x, y, z, 1))
        decode_rows()

    @pl.when(jnp.logical_not(((z == 0) & (h == 1)) | is_root))
    def _():
        relay_factor(0, NCHUNK)

    for i in range(1, NX):
        frm = lax.rem(x + i, NX)
        drain(group(frm), cx_r.at[frm])

    @pl.when((q == 1) & (k != 0))
    def _():
        drain(brow, rf_r)

    @pl.when((h == 1) & (z != 0))
    def _():
        drain(coded, rf_r)
        decode_rows()

    winv = w[...]
    pcol = [nt(bcol[s], winv) for s in range(2)]

    def update(t, c):
        panel = nt(brow[t], winv)
        first = (k == 0) & (t == 0)
        for s in range(2):
            tile = asm[s, t] - nt(panel, pcol[s])
            tile = jnp.where(first, 0.0, tile)
            if s == 0:
                tile = jnp.where(q == 0, panel, tile)
            start = t * (TILE * 4) + 2 * s
            out[pl.ds(start, TILE, stride=4), :] = tile[:, :128]
            out[pl.ds(start + 1, TILE, stride=4), :] = tile[:, 128:]
        return c

    lax.fori_loop(0, TR, update, 0)

    @pl.when(is_root)
    def _():
        ii = lax.broadcasted_iota(jnp.int32, (TILE, TILE), 0)
        jj = lax.broadcasted_iota(jnp.int32, (TILE, TILE), 1)
        factor = jnp.where(ii >= jj, u_ref[...].T, 0.0)
        out[pl.ds(0, TILE, stride=4), :] = factor[:, :128]
        out[pl.ds(1, TILE, stride=4), :] = factor[:, 128:]

    for i in range(1, NX):
        drain(stage.at[0], ch_s.at[i])

    def each(count, view, sem):
        def one(i, c):
            drain(view, sem)
            return c
        lax.fori_loop(0, count, one, 0)

    @pl.when((q == 0) & (k != 0))
    def _():
        each(jnp.where(k == NCOL, OWNERS - 1, OWNERS), brow.at[0, 0:PIECE, :], cs_s)

    each(NY - 1, bcol.at[:, 0:PIECE, :], cy_s)
    each(NX - 1, bcol.at[:, 0:GROUP, :], cx_s)

    @pl.when(((q == 0) & (k != 0)) | is_helper)
    def _():
        each(NZ - 1, coded.at[0], rs_s)
        each(NZ - 1, coded.at[0], ra_s)

    @pl.when((h == 0) & (z != 0))
    def _():
        each(NZ - 2, coded.at[0], ra_s)
        drain(coded, rf_s)

    @pl.when(q == 0)
    def _():
        drain(brow, rf_s)

    sent = (
        jnp.where((h == 1) & (k == 0) & (z == 0), NX - 1, 0)
        + jnp.where((h == 1) & (y == 0) & (z == 0), NY - 1, 0)
        + jnp.where((h == 1) & (z == 0), NZ - 1, 0)
        + jnp.where((h == 1) & jnp.logical_not(is_helper), 1, 0)
        + jnp.where(is_root, 1, 0)
    )
    for i in range(NCHUNK):
        each(sent, part(i), w_s)


def local(front_tiles, child_tiles, target_rows, target_cols, live_counts):
    front = front_tiles.reshape(TR * TILE * 4, 128)
    child = child_tiles.reshape(SLOTS, TILE, TILE)
    hbm = pl.BlockSpec(memory_space=pltpu.HBM)
    dma = pltpu.SemaphoreType.DMA
    out = pl.pallas_call(
        kernel,
        out_shape=pltpu.VMEM(front.shape, F32),
        in_specs=[hbm] * 5,
        out_specs=pl.BlockSpec(memory_space=pltpu.VMEM),
        scratch_shapes=[
            pltpu.VMEM(front.shape, F32),
            pltpu.VMEM(child.shape, BF16),
            pltpu.SMEM((SLOTS,), jnp.int32),
            pltpu.SMEM((SLOTS,), jnp.int32),
            pltpu.SMEM((1,), jnp.int32),
            dma((5,)),
            pltpu.VMEM((NX, STAGE_ROWS, TILE), BF16),
            pltpu.VMEM((NX, STAGE_ROWS, TILE), BF16),
            pltpu.VMEM((2, TR, TILE, TILE), F32),
            pltpu.VMEM((TR, TILE, TILE), F32),
            pltpu.VMEM((NZ, CODED_ROWS, TILE), jnp.int16),
            pltpu.VMEM((2, TILE, TILE), F32),
            pltpu.VMEM((TILE, TILE), F32),
            pltpu.VMEM((TILE, 2 * TILE), F32),
            pltpu.VMEM((TILE, TILE), F32),
            dma((NX,)), dma((NX,)),
            dma, dma((2,)),
            dma, dma,
            dma, dma((NX,)),
            dma, dma,
            dma, dma((NZ,)),
            dma, dma,
            dma, dma((NCHUNK,)),
            pltpu.SemaphoreType.REGULAR,
        ],
        compiler_params=pltpu.CompilerParams(
            collective_id=0, has_side_effects=True, vmem_limit_bytes=56 * 1024 * 1024
        ),
        cost_estimate=pl.CostEstimate(flops=11 * 2 * TILE**3, bytes_accessed=4 * 1024 * 1024, transcendentals=0),
        name="front_panel",
    )(front, child, target_rows.reshape(SLOTS), target_cols.reshape(SLOTS), live_counts.reshape(1))
    return out.reshape(front_tiles.shape)


def solution(mesh):
    placed = (
        P(None, ("cube", "row"), None, None, "col", None),
        P("cube", "row", "col", None, None, None),
        P("cube", "row", "col", None),
        P("cube", "row", "col", None),
        P("cube", "row", "col"),
    )
    return jax.shard_map(
        local,
        mesh=mesh,
        in_specs=placed,
        out_specs=P(None, ("cube", "row"), None, None, "col", None),
        check_vma=False,
    )
```

```python
import jax
import jax.numpy as jnp
from jax import lax
from jax.experimental import pallas as pl
from jax.experimental.pallas import tpu as pltpu
from jax.sharding import PartitionSpec as P

MESH = pl.DeviceIdType.MESH
HIGHEST = lax.Precision.HIGHEST
F32 = jnp.float32
BF16 = jnp.bfloat16

NX, NY, NZ = 4, 8, 8
OWNERS = NX * NY
NCOL = 2 * NZ
TILE = 256
TR = 3
SLOTS = 4
LANES = 2
META = LANES * TILE
STAGE_ROWS = META + 16
PIECE = 2 * TILE // OWNERS
GROUP = PIECE * NY
HALF = TILE // 2
ZPIECE = TILE // NZ
CODED_ROWS = TR * ZPIECE + 16
LIMIT, STEPS = 80.0, 32767.0
NB = 32
NBLOCK = TILE // NB
AWAY_X = list(range(1, NX))
AWAY_Y = list(range(1, NY))
AWAY_Z = list(range(1, NZ))
CHUNKS = ((0, 128, 128), (128, 64, 256), (192, 32, 256), (224, 32, 256))
NCHUNK = len(CHUNKS)


def nt(a, b):
    return lax.dot_general(a, b, (((1,), (1,)), ((), ())), precision=lax.Precision.HIGH, preferred_element_type=F32)


def drain(view, sem, times=1):
    for _ in range(times):
        pltpu.make_async_copy(view, view, sem).wait()


def cholesky_step(b, m_ref, u_ref, w_ref):
    row0 = pl.multiple_of(b * NB, NB)
    block = m_ref[pl.ds(row0, NB), :]
    half = jnp.where(b < NBLOCK // 2, block[:, :128], block[:, 128:256])
    diag = pltpu.roll(half, lax.rem(128 - lax.rem(b * NB, 128), 128), 1)
    left = b < NBLOCK // 2
    shared = jnp.where(left, block[:, :128], block[:, 384:])
    parts = [shared, block[:, 128:256], block[:, 256:384], diag]
    first_rows = lax.broadcasted_iota(jnp.int32, (8, 128), 0)
    done = [[] for _ in parts]
    for g in range(NB // 8):
        more = NB - 8 * g - 8
        cols = [jnp.broadcast_to(parts[3][:, 8 * g + j : 8 * g + j + 1], (more + 8, 128)) for j in range(8)]
        head = [p[:8] for p in parts]
        tail = [p[8:] for p in parts]
        for kk in range(8):
            pivot = cols[kk][kk : kk + 1, :]
            inv = lax.rsqrt(pivot)
            col = cols[kk] * inv
            for j in range(kk + 1, 8):
                cols[j] = cols[j] - col * col[j : j + 1, :]
            masked = jnp.where(first_rows > kk, col[:8], 0.0)
            for i in range(len(parts)):
                top = head[i][kk : kk + 1, :] * inv
                head[i] = jnp.where(first_rows == kk, top, head[i] - masked * top)
                if more:
                    tail[i] = tail[i] - col[8:] * top
        for i in range(len(parts)):
            done[i].append(head[i])
        parts = tail
    shared, u_right, w_left = [jnp.concatenate(d, axis=0) for d in done[:3]]
    zero = jnp.zeros_like(shared)
    both = jnp.concatenate([jnp.where(left, shared, zero), u_right, w_left, jnp.where(left, zero, shared)], axis=1)
    u_ref[pl.ds(row0, NB), :] = both[:, :TILE]
    w_ref[pl.ds(row0, NB), :] = both[:, TILE:]
    b1 = both.astype(BF16)
    rest = both - b1.astype(F32)
    b2 = rest.astype(BF16)
    b3 = (rest - b2.astype(F32)).astype(BF16)
    a1, a2, a3 = b1[:, :TILE], b2[:, :TILE], b3[:, :TILE]
    lhs = jnp.concatenate([a1, a1, a2, a2, a1, a3], axis=0)
    rhs = jnp.concatenate([b1, b2, b1, b2, b3, b1], axis=0)
    m_ref[...] -= lax.dot_general(lhs, rhs, (((0,), (0,)), ((), ())), preferred_element_type=F32)


def kernel(
    front_h, child_h, trow_h, tcol_h, live_h, out,
    front, child, trow, tcol, live, in_s, stage, recv, asm, brow, coded, col_out, col_in, col, bcol, w, m_ref, u_ref,
    ch_s, ch_r, cs_s, cs_r, cy_s, cy_r, cx_s, cx_r, rs_s, rs_r, ra_s, ra_r, rf_s, rf_r, w_s, w_r, go,
):
    x, y, q = lax.axis_index("cube"), lax.axis_index("row"), lax.axis_index("col")
    z, h = q // 2, q % 2
    k = x * NY + y
    is_root = (k == 0) & (q == 0)
    is_helper = (k == 0) & (q == 1)

    loads = [
        pltpu.make_async_copy(src, dst, in_s.at[i])
        for i, (src, dst) in enumerate(
            [(trow_h, trow), (tcol_h, tcol), (live_h, live), (child_h, child), (front_h, front)]
        )
    ]
    for load in loads:
        load.start()

    def at(xx, yy, zz, hh):
        return (xx, yy, zz * 2 + hh)

    def send(src, dst, ssem, rsem, device):
        pltpu.make_async_remote_copy(
            src_ref=src, dst_ref=dst, send_sem=ssem, recv_sem=rsem, device_id=device, device_id_type=MESH
        ).start()

    my_s, my_q = k // NCOL, k % NCOL
    my_z, my_h = my_q // 2, my_q % 2

    barrier = pltpu.get_barrier_semaphore()

    def greet(device):
        pl.semaphore_signal(barrier, inc=1, device_id=device, device_id_type=MESH)

    def greet_plane(i, c):
        p = lax.rem(k + i, OWNERS)
        greet(at(p // NY, lax.rem(p, NY), z, h))
        return c

    def greet_z(i, c):
        greet(at(x, y, lax.rem(z + i, NZ), h))
        return c

    lax.fori_loop(1, NX * NY, greet_plane, 0)
    lax.fori_loop(1, NZ, greet_z, 0)
    greet(at(x, y, z, 1 - h))

    @pl.when((q == 0) & (my_h == 1) & (my_z != 0))
    def _():
        greet(at(x, y, my_z, my_h))

    speaks = (my_q == q) & (q != 0)

    for load in loads[:4]:
        load.wait()
    alive = [jnp.where(m < live[0], 1, 0) for m in range(SLOTS)]
    cube_of = [lax.rem(trow[m], OWNERS) // NY for m in range(SLOTS)]
    tile_of = [(trow[m] // OWNERS) * 2 + tcol[m] // NCOL for m in range(SLOTS)]
    meta_row = lax.broadcasted_iota(jnp.int32, (16, TILE), 0)
    for d in range(NX):
        seen = 0
        index = [0, 0]
        label = [-1, -1]
        for m in range(SLOTS):
            hit = alive[m] * jnp.where(cube_of[m] == d, 1, 0)
            for lane in range(LANES):
                here = hit * jnp.where(seen == lane, 1, 0)
                index[lane] = index[lane] + here * m
                label[lane] = label[lane] + here * (tile_of[m] + 1)
            seen = seen + hit
        for lane in range(LANES):
            stage[d, lane * TILE : (lane + 1) * TILE, :] = child[index[lane]]
        tags = jnp.where(meta_row == 0, label[0], jnp.where(meta_row == 1, label[1], -1))
        stage[d, META:, :] = tags.astype(F32).astype(BF16)

    w[: TILE // 2, TILE // 2 :] = jnp.zeros((TILE // 2, TILE // 2), F32)

    loads[4].wait()
    pl.semaphore_wait(barrier, NX * NY - 1 + NZ - 1 + 1 + jnp.where(speaks & (h == 1) & (z != 0), 1, 0))

    @pl.when(speaks)
    def _():
        pl.semaphore_signal(go, inc=1, device_id=at(x, y, 0, 0), device_id_type=MESH)

    for i in AWAY_X:
        d = lax.rem(x + i, NX)
        send(stage.at[d], recv.at[x], ch_s.at[i], ch_r.at[x], at(d, y, z, h))
    recv[x] = stage[x]

    def wait_children():
        for i in range(1, NX):
            src = lax.rem(x + i, NX)
            drain(recv.at[src], ch_r.at[src])

    def assemble(t, s, dst):
        tile_id = (t * 2 + s).astype(F32) if hasattr(t, "astype") else float(t * 2 + s)
        masks = []
        for src in range(NX):
            tags = recv[src, META:, :].astype(F32)
            masks.append([tags[lane : lane + 1, :] == tile_id for lane in range(LANES)])

        def rows(i, c):
            r0 = pl.multiple_of(i * 32, 32)
            start = t * (TILE * 4) + i * 128 + 2 * s
            acc = jnp.concatenate(
                [front[pl.ds(start, 32, stride=4), :], front[pl.ds(start + 1, 32, stride=4), :]], axis=1
            )
            for src in range(NX):
                for lane in range(LANES):
                    v = recv[src, pl.ds(lane * TILE + r0, 32), :].astype(F32)
                    acc = acc + jnp.where(masks[src][lane], v, 0.0)
            dst[pl.ds(r0, 32), :] = acc
            return c

        lax.fori_loop(0, TILE // 32, rows, 0)

    def part(i):
        row0, rows, width = CHUNKS[i]
        return w.at[row0 : row0 + rows, 0:width]

    def relay_factor(first, last):
        for i in range(first, last):
            drain(part(i), w_r.at[i])

            def pass_on(*device):
                send(part(i), part(i), w_s, w_r.at[i], at(*device))

            @pl.when(is_helper)
            def _():
                for j in AWAY_X:
                    pass_on(j, 0, 0, 1)

            @pl.when((y == 0) & (z == 0) & (h == 1))
            def _():
                for j in AWAY_Y:
                    pass_on(x, j, 0, 1)

            @pl.when((z == 0) & (h == 1))
            def _():
                for j in AWAY_Z:
                    pass_on(x, y, j, 1)

            @pl.when((h == 1) & jnp.logical_not(is_helper))
            def _():
                pass_on(x, y, z, 0)

    def encode(v):
        return ((v + (STEPS + 1.5)).astype(jnp.int32) - int(STEPS + 1)).astype(jnp.int16)

    def level_of(t):
        peak = jnp.max(jnp.max(jnp.abs(brow[t]), axis=0, keepdims=True), axis=1, keepdims=True)
        return jnp.broadcast_to(jnp.floor(peak * (STEPS / LIMIT)) + 1.0, (1, TILE))

    def encode_column():
        level = level_of(0)[:, :HALF]
        inverse = (STEPS * STEPS / LIMIT) / level
        tags = jnp.broadcast_to(level, (PIECE, HALF)).astype(jnp.int32).astype(jnp.int16)

        def one(i, c):
            view = pl.ds(pl.multiple_of(i * PIECE, PIECE), PIECE)
            for side in range(2):
                at_piece = side * (OWNERS // 2) + i
                v = brow[0, view, side * HALF : (side + 1) * HALF]
                col_out[at_piece, 0:PIECE, :] = encode(v * inverse)
                col_out[at_piece, PIECE:, :] = tags
            return c

        lax.fori_loop(0, OWNERS // 2, one, 0)

    def decode_columns():
        for s in range(2):
            tags = col_in[s, PIECE:, :].astype(jnp.int32).astype(F32)[0:1, :] * (LIMIT / (STEPS * STEPS))
            for side in range(2):
                v = col[s, side * TILE : (side + 1) * TILE, :].astype(jnp.int32).astype(F32)
                bcol[s, :, side * HALF : (side + 1) * HALF] = v * tags

    def encode_rows():
        tag_row = lax.broadcasted_iota(jnp.int32, (16, TILE), 0)
        tags = jnp.zeros((16, TILE), F32)
        inverse = []
        for t in range(TR):
            level = level_of(t)
            tags = jnp.where(tag_row == t, level, tags)
            inverse.append((STEPS * STEPS / LIMIT) / level)

        def one(p, c):
            view = pl.ds(pl.multiple_of(p * ZPIECE, ZPIECE), ZPIECE)
            for t in range(TR):
                coded[p, t * ZPIECE : (t + 1) * ZPIECE, :] = encode(brow[t, view, :] * inverse[t])
            coded[p, TR * ZPIECE :, :] = tags.astype(jnp.int32).astype(jnp.int16)
            return c

        lax.fori_loop(0, NZ, one, 0)

    def decode_rows():
        def one(p, c):
            view = pl.ds(pl.multiple_of(p * ZPIECE, ZPIECE), ZPIECE)
            tags = coded[p, TR * ZPIECE :, :].astype(jnp.int32).astype(F32) * (LIMIT / (STEPS * STEPS))
            for t in range(TR):
                v = coded[p, t * ZPIECE : (t + 1) * ZPIECE, :].astype(jnp.int32).astype(F32)
                brow[t, view, :] = v * tags[t : t + 1, :]
            return c

        lax.fori_loop(0, NZ, one, 0)

    def spread_rows():
        encode_rows()

        for p in AWAY_Z:
            send(coded.at[p], coded.at[p], rs_s, rs_r, at(x, y, p, 0))
        for p in AWAY_Z:
            send(coded.at[0], coded.at[0], ra_s, ra_r.at[0], at(x, y, p, 0))

    @pl.when(q == 0)
    def _():
        wait_children()
        assemble(0, 0, brow.at[0])
        @pl.when(k != 0)
        def _():
            encode_column()

        @pl.when(my_q != 0)
        def _():
            pl.semaphore_wait(go, 1)

        @pl.when(k != 0)
        def _():
            def scatter(p, c):
                @pl.when((p != k) | (my_q != 0))
                def _():
                    send(col_out.at[p], col_in.at[my_s], cs_s, cs_r.at[my_s],
                         at(p // NY, lax.rem(p, NY), my_z, my_h))
                return c

            lax.fori_loop(0, OWNERS, scatter, 0)

        @pl.when(k == NCOL)
        def _():
            col_in[1] = col_out[NCOL]

        for t in range(1, TR):
            assemble(t, 0, brow.at[t])

        send(brow, brow, rf_s, rf_r, at(x, y, 0, 1))

        @pl.when(k != 0)
        def _():
            spread_rows()

    @pl.when(is_root)
    def _():
        a = brow[0]
        m_ref[:, :TILE] = 0.5 * (a + a.T)
        ii = lax.broadcasted_iota(jnp.int32, (TILE, TILE), 0)
        jj = lax.broadcasted_iota(jnp.int32, (TILE, TILE), 1)
        m_ref[:, TILE:] = jnp.where(ii == jj, 1.0, 0.0)

        def step(b, c):
            cholesky_step(b, m_ref, u_ref, w)
            for i in range(NCHUNK):
                @pl.when(b == (CHUNKS[i][0] + CHUNKS[i][1]) // NB - 1)
                def _():
                    send(part(i), part(i), w_s, w_r.at[i], at(0, 0, 0, 1))
            return c

        lax.fori_loop(0, NBLOCK, step, 0)

    @pl.when(is_helper)
    def _():
        drain(brow, rf_r)
        spread_rows()

    @pl.when(q != 0)
    def _():
        drain(col_in.at[0], cs_r.at[0])

    @pl.when(jnp.logical_not((q == 0) & (k == NCOL)))
    def _():
        drain(col_in.at[1], cs_r.at[1])

    mine = pl.ds(pl.multiple_of(k * PIECE, PIECE), PIECE)
    for s in range(2):
        col[s, mine, :] = col_in[s, 0:PIECE, :]
    for i in AWAY_Y:
        send(col.at[:, mine, :], col.at[:, mine, :], cy_s, cy_r, at(x, lax.rem(y + i, NY), z, h))

    def group(i):
        return col.at[:, pl.ds(pl.multiple_of(i * GROUP, GROUP), GROUP), :]

    def gather_columns():
        drain(col.at[:, 0 : GROUP - PIECE, :], cy_r)
        for i in AWAY_X:
            send(group(x), group(x), cx_s, cx_r.at[x], at(lax.rem(x + i, NX), y, z, h))

    early = (y == 0) & (z == 0) & (h == 1)
    middle = (y != 0) & (z == 0) & (h == 1)

    @pl.when((h == 0) & (z != 0))
    def _():
        drain(coded.at[0], rs_r)

        for i in AWAY_Z:
            to = lax.rem(z + i, NZ)
            @pl.when(to != 0)
            def _():
                send(coded.at[z], coded.at[z], ra_s, ra_r.at[z], at(x, y, to, 0))

    @pl.when(early)
    def _():
        relay_factor(0, NCHUNK)
        gather_columns()

    @pl.when(middle)
    def _():
        relay_factor(0, 1)
        gather_columns()
        relay_factor(1, NCHUNK)

    @pl.when((z != 0) | (h == 0))
    def _():
        gather_columns()

    @pl.when(q != 0)
    def _():
        wait_children()

        def all_rows(t, c):
            assemble(t, 0, asm.at[0, t])
            return c

        lax.fori_loop(0, TR, all_rows, 0)

    def second_rows(t, c):
        assemble(t, 1, asm.at[1, t])
        return c

    lax.fori_loop(0, TR, second_rows, 0)

    @pl.when((h == 0) & (z != 0))
    def _():
        def one(i, c):
            frm = lax.rem(z + i, NZ)
            drain(coded.at[0], ra_r.at[frm])
            return c

        lax.fori_loop(1, NZ, one, 0)
        send(coded, coded, rf_s, rf_r, at(x, y, z, 1))
        decode_rows()

    @pl.when(jnp.logical_not(((z == 0) & (h == 1)) | is_root))
    def _():
        relay_factor(0, NCHUNK)

    for i in range(1, NX):
        frm = lax.rem(x + i, NX)
        drain(group(frm), cx_r.at[frm])
    decode_columns()

    @pl.when((q == 1) & (k != 0))
    def _():
        drain(brow, rf_r)

    @pl.when((h == 1) & (z != 0))
    def _():
        drain(coded, rf_r)
        decode_rows()

    winv = w[...]
    pcol = [nt(bcol[s], winv) for s in range(2)]

    def update(t, c):
        panel = nt(brow[t], winv)
        first = (k == 0) & (t == 0)
        for s in range(2):
            tile = asm[s, t] - nt(panel, pcol[s])
            tile = jnp.where(first, 0.0, tile)
            if s == 0:
                tile = jnp.where(q == 0, panel, tile)
            start = t * (TILE * 4) + 2 * s
            out[pl.ds(start, TILE, stride=4), :] = tile[:, :128]
            out[pl.ds(start + 1, TILE, stride=4), :] = tile[:, 128:]
        return c

    lax.fori_loop(0, TR, update, 0)

    @pl.when(is_root)
    def _():
        ii = lax.broadcasted_iota(jnp.int32, (TILE, TILE), 0)
        jj = lax.broadcasted_iota(jnp.int32, (TILE, TILE), 1)
        factor = jnp.where(ii >= jj, u_ref[...].T, 0.0)
        out[pl.ds(0, TILE, stride=4), :] = factor[:, :128]
        out[pl.ds(1, TILE, stride=4), :] = factor[:, 128:]

    for i in range(1, NX):
        drain(stage.at[0], ch_s.at[i])

    def each(count, view, sem):
        def one(i, c):
            drain(view, sem)
            return c
        lax.fori_loop(0, count, one, 0)

    @pl.when((q == 0) & (k != 0))
    def _():
        each(jnp.where(k == NCOL, OWNERS - 1, OWNERS), col_out.at[0], cs_s)

    each(NY - 1, col.at[:, 0:PIECE, :], cy_s)
    each(NX - 1, col.at[:, 0:GROUP, :], cx_s)

    @pl.when(((q == 0) & (k != 0)) | is_helper)
    def _():
        each(NZ - 1, coded.at[0], rs_s)
        each(NZ - 1, coded.at[0], ra_s)

    @pl.when((h == 0) & (z != 0))
    def _():
        each(NZ - 2, coded.at[0], ra_s)
        drain(coded, rf_s)

    @pl.when(q == 0)
    def _():
        drain(brow, rf_s)

    sent = (
        jnp.where((h == 1) & (k == 0) & (z == 0), NX - 1, 0)
        + jnp.where((h == 1) & (y == 0) & (z == 0), NY - 1, 0)
        + jnp.where((h == 1) & (z == 0), NZ - 1, 0)
        + jnp.where((h == 1) & jnp.logical_not(is_helper), 1, 0)
        + jnp.where(is_root, 1, 0)
    )
    for i in range(NCHUNK):
        each(sent, part(i), w_s)


def local(front_tiles, child_tiles, target_rows, target_cols, live_counts):
    front = front_tiles.reshape(TR * TILE * 4, 128)
    child = child_tiles.reshape(SLOTS, TILE, TILE)
    hbm = pl.BlockSpec(memory_space=pltpu.HBM)
    dma = pltpu.SemaphoreType.DMA
    out = pl.pallas_call(
        kernel,
        out_shape=pltpu.VMEM(front.shape, F32),
        in_specs=[hbm] * 5,
        out_specs=pl.BlockSpec(memory_space=pltpu.VMEM),
        scratch_shapes=[
            pltpu.VMEM(front.shape, F32),
            pltpu.VMEM(child.shape, BF16),
            pltpu.SMEM((SLOTS,), jnp.int32),
            pltpu.SMEM((SLOTS,), jnp.int32),
            pltpu.SMEM((1,), jnp.int32),
            dma((5,)),
            pltpu.VMEM((NX, STAGE_ROWS, TILE), BF16),
            pltpu.VMEM((NX, STAGE_ROWS, TILE), BF16),
            pltpu.VMEM((2, TR, TILE, TILE), F32),
            pltpu.VMEM((TR, TILE, TILE), F32),
            pltpu.VMEM((NZ, CODED_ROWS, TILE), jnp.int16),
            pltpu.VMEM((OWNERS, 2 * PIECE, HALF), jnp.int16),
            pltpu.VMEM((2, 2 * PIECE, HALF), jnp.int16),
            pltpu.VMEM((2, 2 * TILE, HALF), jnp.int16),
            pltpu.VMEM((2, TILE, TILE), F32),
            pltpu.VMEM((TILE, TILE), F32),
            pltpu.VMEM((TILE, 2 * TILE), F32),
            pltpu.VMEM((TILE, TILE), F32),
            dma((NX,)), dma((NX,)),
            dma, dma((2,)),
            dma, dma,
            dma, dma((NX,)),
            dma, dma,
            dma, dma((NZ,)),
            dma, dma,
            dma, dma((NCHUNK,)),
            pltpu.SemaphoreType.REGULAR,
        ],
        compiler_params=pltpu.CompilerParams(
            collective_id=0, has_side_effects=True, vmem_limit_bytes=56 * 1024 * 1024
        ),
        cost_estimate=pl.CostEstimate(flops=11 * 2 * TILE**3, bytes_accessed=4 * 1024 * 1024, transcendentals=0),
        name="front_panel",
    )(front, child, target_rows.reshape(SLOTS), target_cols.reshape(SLOTS), live_counts.reshape(1))
    return out.reshape(front_tiles.shape)


def solution(mesh):
    placed = (
        P(None, ("cube", "row"), None, None, "col", None),
        P("cube", "row", "col", None, None, None),
        P("cube", "row", "col", None),
        P("cube", "row", "col", None),
        P("cube", "row", "col"),
    )
    return jax.shard_map(
        local,
        mesh=mesh,
        in_specs=placed,
        out_specs=P(None, ("cube", "row"), None, None, "col", None),
        check_vma=False,
    )
```

```python
import jax
import jax.numpy as jnp
from jax import lax
from jax.experimental import pallas as pl
from jax.experimental.pallas import tpu as pltpu
from jax.sharding import PartitionSpec as P

MESH = pl.DeviceIdType.MESH
HIGHEST = lax.Precision.HIGHEST
F32 = jnp.float32
BF16 = jnp.bfloat16

NX, NY, NZ = 4, 8, 8
OWNERS = NX * NY
NCOL = 2 * NZ
TILE = 256
TR = 3
SLOTS = 4
LANES = 2
META = LANES * TILE
STAGE_ROWS = META + 16
PIECE = 2 * TILE // OWNERS
GROUP = PIECE * NY
HALF = TILE // 2
ZPIECE = TILE // NZ
CODED_ROWS = TR * ZPIECE + 16
LIMIT, STEPS = 80.0, 32767.0
NB = 32
NBLOCK = TILE // NB
AWAY_X = list(range(1, NX))
AWAY_Y = list(range(1, NY))
AWAY_Z = list(range(1, NZ))
CHUNKS = ((0, 128, 128), (128, 32, 256), (160, 32, 256), (192, 32, 256), (224, 32, 256))
NCHUNK = len(CHUNKS)


def nt(a, b):
    return lax.dot_general(a, b, (((1,), (1,)), ((), ())), precision=lax.Precision.HIGH, preferred_element_type=F32)


def drain(view, sem, times=1):
    for _ in range(times):
        pltpu.make_async_copy(view, view, sem).wait()


def cholesky_step(b, m_ref, u_ref, w_ref):
    row0 = pl.multiple_of(b * NB, NB)
    block = m_ref[pl.ds(row0, NB), :]
    half = jnp.where(b < NBLOCK // 2, block[:, :128], block[:, 128:256])
    diag = pltpu.roll(half, lax.rem(128 - lax.rem(b * NB, 128), 128), 1)
    left = b < NBLOCK // 2
    shared = jnp.where(left, block[:, :128], block[:, 384:])
    parts = [shared, block[:, 128:256], block[:, 256:384], diag]
    first_rows = lax.broadcasted_iota(jnp.int32, (8, 128), 0)
    done = [[] for _ in parts]
    for g in range(NB // 8):
        more = NB - 8 * g - 8
        cols = [jnp.broadcast_to(parts[3][:, 8 * g + j : 8 * g + j + 1], (more + 8, 128)) for j in range(8)]
        head = [p[:8] for p in parts]
        tail = [p[8:] for p in parts]
        for kk in range(8):
            pivot = cols[kk][kk : kk + 1, :]
            inv = lax.rsqrt(pivot)
            col = cols[kk] * inv
            for j in range(kk + 1, 8):
                cols[j] = cols[j] - col * col[j : j + 1, :]
            masked = jnp.where(first_rows > kk, col[:8], 0.0)
            for i in range(len(parts)):
                top = head[i][kk : kk + 1, :] * inv
                head[i] = jnp.where(first_rows == kk, top, head[i] - masked * top)
                if more:
                    tail[i] = tail[i] - col[8:] * top
        for i in range(len(parts)):
            done[i].append(head[i])
        parts = tail
    shared, u_right, w_left = [jnp.concatenate(d, axis=0) for d in done[:3]]
    zero = jnp.zeros_like(shared)
    both = jnp.concatenate([jnp.where(left, shared, zero), u_right, w_left, jnp.where(left, zero, shared)], axis=1)
    u_ref[pl.ds(row0, NB), :] = both[:, :TILE]
    w_ref[pl.ds(row0, NB), :] = both[:, TILE:]
    b1 = both.astype(BF16)
    rest = both - b1.astype(F32)
    b2 = rest.astype(BF16)
    b3 = (rest - b2.astype(F32)).astype(BF16)
    a1, a2, a3 = b1[:, :TILE], b2[:, :TILE], b3[:, :TILE]
    lhs = jnp.concatenate([a1, a1, a2, a2, a1, a3], axis=0)
    rhs = jnp.concatenate([b1, b2, b1, b2, b3, b1], axis=0)
    m_ref[...] -= lax.dot_general(lhs, rhs, (((0,), (0,)), ((), ())), preferred_element_type=F32)


def kernel(
    front_h, child_h, trow_h, tcol_h, live_h, out,
    front, child, trow, tcol, live, in_s, stage, recv, asm, brow, coded, col_out, col_in, col, bcol, w, m_ref, u_ref,
    ch_s, ch_r, cs_s, cs_r, cy_s, cy_r, cx_s, cx_r, rs_s, rs_r, ra_s, ra_r, rf_s, rf_r, w_s, w_r, go,
):
    x, y, q = lax.axis_index("cube"), lax.axis_index("row"), lax.axis_index("col")
    z, h = q // 2, q % 2
    k = x * NY + y
    is_root = (k == 0) & (q == 0)
    is_helper = (k == 0) & (q == 1)

    loads = [
        pltpu.make_async_copy(src, dst, in_s.at[i])
        for i, (src, dst) in enumerate(
            [(trow_h, trow), (tcol_h, tcol), (live_h, live), (child_h, child), (front_h, front)]
        )
    ]
    for load in loads:
        load.start()

    def at(xx, yy, zz, hh):
        return (xx, yy, zz * 2 + hh)

    def send(src, dst, ssem, rsem, device):
        pltpu.make_async_remote_copy(
            src_ref=src, dst_ref=dst, send_sem=ssem, recv_sem=rsem, device_id=device, device_id_type=MESH
        ).start()

    my_s, my_q = k // NCOL, k % NCOL
    my_z, my_h = my_q // 2, my_q % 2

    barrier = pltpu.get_barrier_semaphore()

    def greet(device):
        pl.semaphore_signal(barrier, inc=1, device_id=device, device_id_type=MESH)

    def greet_plane(i, c):
        p = lax.rem(k + i, OWNERS)
        greet(at(p // NY, lax.rem(p, NY), z, h))
        return c

    def greet_z(i, c):
        greet(at(x, y, lax.rem(z + i, NZ), h))
        return c

    lax.fori_loop(1, NX * NY, greet_plane, 0)
    lax.fori_loop(1, NZ, greet_z, 0)
    greet(at(x, y, z, 1 - h))

    @pl.when((q == 0) & (my_h == 1) & (my_z != 0))
    def _():
        greet(at(x, y, my_z, my_h))

    speaks = (my_q == q) & (q != 0)

    for load in loads[:4]:
        load.wait()
    alive = [jnp.where(m < live[0], 1, 0) for m in range(SLOTS)]
    cube_of = [lax.rem(trow[m], OWNERS) // NY for m in range(SLOTS)]
    tile_of = [(trow[m] // OWNERS) * 2 + tcol[m] // NCOL for m in range(SLOTS)]
    meta_row = lax.broadcasted_iota(jnp.int32, (16, TILE), 0)
    for d in range(NX):
        seen = 0
        index = [0, 0]
        label = [-1, -1]
        for m in range(SLOTS):
            hit = alive[m] * jnp.where(cube_of[m] == d, 1, 0)
            for lane in range(LANES):
                here = hit * jnp.where(seen == lane, 1, 0)
                index[lane] = index[lane] + here * m
                label[lane] = label[lane] + here * (tile_of[m] + 1)
            seen = seen + hit
        for lane in range(LANES):
            stage[d, lane * TILE : (lane + 1) * TILE, :] = child[index[lane]]
        tags = jnp.where(meta_row == 0, label[0], jnp.where(meta_row == 1, label[1], -1))
        stage[d, META:, :] = tags.astype(F32).astype(BF16)

    w[: TILE // 2, TILE // 2 :] = jnp.zeros((TILE // 2, TILE // 2), F32)

    loads[4].wait()
    pl.semaphore_wait(barrier, NX * NY - 1 + NZ - 1 + 1 + jnp.where(speaks & (h == 1) & (z != 0), 1, 0))

    @pl.when(speaks)
    def _():
        pl.semaphore_signal(go, inc=1, device_id=at(x, y, 0, 0), device_id_type=MESH)

    for i in AWAY_X:
        d = lax.rem(x + i, NX)
        send(stage.at[d], recv.at[x], ch_s.at[i], ch_r.at[x], at(d, y, z, h))
    recv[x] = stage[x]

    def wait_children():
        for i in range(1, NX):
            src = lax.rem(x + i, NX)
            drain(recv.at[src], ch_r.at[src])

    def assemble(t, s, dst):
        tile_id = (t * 2 + s).astype(F32) if hasattr(t, "astype") else float(t * 2 + s)
        masks = []
        for src in range(NX):
            tags = recv[src, META:, :].astype(F32)
            masks.append([tags[lane : lane + 1, :] == tile_id for lane in range(LANES)])

        def rows(i, c):
            r0 = pl.multiple_of(i * 32, 32)
            start = t * (TILE * 4) + i * 128 + 2 * s
            acc = jnp.concatenate(
                [front[pl.ds(start, 32, stride=4), :], front[pl.ds(start + 1, 32, stride=4), :]], axis=1
            )
            for src in range(NX):
                for lane in range(LANES):
                    v = recv[src, pl.ds(lane * TILE + r0, 32), :].astype(F32)
                    acc = acc + jnp.where(masks[src][lane], v, 0.0)
            dst[pl.ds(r0, 32), :] = acc
            return c

        lax.fori_loop(0, TILE // 32, rows, 0)

    def part(i):
        row0, rows, width = CHUNKS[i]
        return w.at[row0 : row0 + rows, 0:width]

    def relay_factor(first, last):
        for i in range(first, last):
            drain(part(i), w_r.at[i])

            def pass_on(*device):
                send(part(i), part(i), w_s, w_r.at[i], at(*device))

            @pl.when((y == 0) & (z == 0) & (h == 1))
            def _():
                for j in AWAY_Y:
                    pass_on(x, j, 0, 1)

            @pl.when((z == 0) & (h == 1))
            def _():
                for j in AWAY_Z:
                    pass_on(x, y, j, 1)

            @pl.when((h == 1) & jnp.logical_not(is_helper))
            def _():
                pass_on(x, y, z, 0)

    def encode(v):
        return ((v + (STEPS + 1.5)).astype(jnp.int32) - int(STEPS + 1)).astype(jnp.int16)

    def level_of(t):
        peak = jnp.max(jnp.max(jnp.abs(brow[t]), axis=0, keepdims=True), axis=1, keepdims=True)
        return jnp.broadcast_to(jnp.floor(peak * (STEPS / LIMIT)) + 1.0, (1, TILE))

    def encode_column():
        level = level_of(0)[:, :HALF]
        inverse = (STEPS * STEPS / LIMIT) / level
        tags = jnp.broadcast_to(level, (PIECE, HALF)).astype(jnp.int32).astype(jnp.int16)

        def one(i, c):
            view = pl.ds(pl.multiple_of(i * PIECE, PIECE), PIECE)
            for side in range(2):
                at_piece = side * (OWNERS // 2) + i
                v = brow[0, view, side * HALF : (side + 1) * HALF]
                col_out[at_piece, 0:PIECE, :] = encode(v * inverse)
                col_out[at_piece, PIECE:, :] = tags
            return c

        lax.fori_loop(0, OWNERS // 2, one, 0)

    def decode_columns():
        for s in range(2):
            tags = col_in[s, PIECE:, :].astype(jnp.int32).astype(F32)[0:1, :] * (LIMIT / (STEPS * STEPS))
            for side in range(2):
                v = col[s, side * TILE : (side + 1) * TILE, :].astype(jnp.int32).astype(F32)
                bcol[s, :, side * HALF : (side + 1) * HALF] = v * tags

    def encode_rows():
        tag_row = lax.broadcasted_iota(jnp.int32, (16, TILE), 0)
        tags = jnp.zeros((16, TILE), F32)
        inverse = []
        for t in range(TR):
            level = level_of(t)
            tags = jnp.where(tag_row == t, level, tags)
            inverse.append((STEPS * STEPS / LIMIT) / level)

        def one(p, c):
            view = pl.ds(pl.multiple_of(p * ZPIECE, ZPIECE), ZPIECE)
            for t in range(TR):
                coded[p, t * ZPIECE : (t + 1) * ZPIECE, :] = encode(brow[t, view, :] * inverse[t])
            coded[p, TR * ZPIECE :, :] = tags.astype(jnp.int32).astype(jnp.int16)
            return c

        lax.fori_loop(0, NZ, one, 0)

    def decode_rows():
        def one(p, c):
            view = pl.ds(pl.multiple_of(p * ZPIECE, ZPIECE), ZPIECE)
            tags = coded[p, TR * ZPIECE :, :].astype(jnp.int32).astype(F32) * (LIMIT / (STEPS * STEPS))
            for t in range(TR):
                v = coded[p, t * ZPIECE : (t + 1) * ZPIECE, :].astype(jnp.int32).astype(F32)
                brow[t, view, :] = v * tags[t : t + 1, :]
            return c

        lax.fori_loop(0, NZ, one, 0)

    def spread_rows():
        encode_rows()

        for p in AWAY_Z:
            send(coded.at[p], coded.at[p], rs_s, rs_r, at(x, y, p, 0))
        for p in AWAY_Z:
            send(coded.at[0], coded.at[0], ra_s, ra_r.at[0], at(x, y, p, 0))

    @pl.when(q == 0)
    def _():
        wait_children()
        assemble(0, 0, brow.at[0])
        @pl.when(k != 0)
        def _():
            encode_column()

        @pl.when(my_q != 0)
        def _():
            pl.semaphore_wait(go, 1)

        @pl.when(k != 0)
        def _():
            def scatter(p, c):
                @pl.when((p != k) | (my_q != 0))
                def _():
                    send(col_out.at[p], col_in.at[my_s], cs_s, cs_r.at[my_s],
                         at(p // NY, lax.rem(p, NY), my_z, my_h))
                return c

            lax.fori_loop(0, OWNERS, scatter, 0)

        @pl.when(k == NCOL)
        def _():
            col_in[1] = col_out[NCOL]

        for t in range(1, TR):
            assemble(t, 0, brow.at[t])

        send(brow, brow, rf_s, rf_r, at(x, y, 0, 1))

        @pl.when(k != 0)
        def _():
            spread_rows()

    @pl.when(is_root)
    def _():
        a = brow[0]
        m_ref[:, :TILE] = 0.5 * (a + a.T)
        ii = lax.broadcasted_iota(jnp.int32, (TILE, TILE), 0)
        jj = lax.broadcasted_iota(jnp.int32, (TILE, TILE), 1)
        m_ref[:, TILE:] = jnp.where(ii == jj, 1.0, 0.0)

        def step(b, c):
            cholesky_step(b, m_ref, u_ref, w)
            for i in range(NCHUNK):
                @pl.when(b == (CHUNKS[i][0] + CHUNKS[i][1]) // NB - 1)
                def _():
                    for j in range(NX):
                        send(part(i), part(i), w_s, w_r.at[i], at(j, 0, 0, 1))
            return c

        lax.fori_loop(0, NBLOCK, step, 0)

    @pl.when(is_helper)
    def _():
        drain(brow, rf_r)
        spread_rows()

    @pl.when(q != 0)
    def _():
        drain(col_in.at[0], cs_r.at[0])

    @pl.when(jnp.logical_not((q == 0) & (k == NCOL)))
    def _():
        drain(col_in.at[1], cs_r.at[1])

    mine = pl.ds(pl.multiple_of(k * PIECE, PIECE), PIECE)
    for s in range(2):
        col[s, mine, :] = col_in[s, 0:PIECE, :]
    for i in AWAY_Y:
        send(col.at[:, mine, :], col.at[:, mine, :], cy_s, cy_r, at(x, lax.rem(y + i, NY), z, h))

    def group(i):
        return col.at[:, pl.ds(pl.multiple_of(i * GROUP, GROUP), GROUP), :]

    def gather_columns():
        drain(col.at[:, 0 : GROUP - PIECE, :], cy_r)
        for i in AWAY_X:
            send(group(x), group(x), cx_s, cx_r.at[x], at(lax.rem(x + i, NX), y, z, h))

    early = (y == 0) & (z == 0) & (h == 1)
    middle = (y != 0) & (z == 0) & (h == 1)

    @pl.when((h == 0) & (z != 0))
    def _():
        drain(coded.at[0], rs_r)

        for i in AWAY_Z:
            to = lax.rem(z + i, NZ)
            @pl.when(to != 0)
            def _():
                send(coded.at[z], coded.at[z], ra_s, ra_r.at[z], at(x, y, to, 0))

    @pl.when(early)
    def _():
        relay_factor(0, NCHUNK)
        gather_columns()

    @pl.when(middle)
    def _():
        relay_factor(0, 2)
        gather_columns()
        relay_factor(2, NCHUNK)

    @pl.when((z != 0) | (h == 0))
    def _():
        gather_columns()

    @pl.when(q != 0)
    def _():
        wait_children()

        def all_rows(t, c):
            assemble(t, 0, asm.at[0, t])
            return c

        lax.fori_loop(0, TR, all_rows, 0)

    def second_rows(t, c):
        assemble(t, 1, asm.at[1, t])
        return c

    lax.fori_loop(0, TR, second_rows, 0)

    @pl.when((h == 0) & (z != 0))
    def _():
        def one(i, c):
            frm = lax.rem(z + i, NZ)
            drain(coded.at[0], ra_r.at[frm])
            return c

        lax.fori_loop(1, NZ, one, 0)
        send(coded, coded, rf_s, rf_r, at(x, y, z, 1))
        decode_rows()

    def finish_columns():
        for i in range(1, NX):
            frm = lax.rem(x + i, NX)
            drain(group(frm), cx_r.at[frm])
        decode_columns()

    @pl.when(h == 0)
    def _():
        finish_columns()

    @pl.when(jnp.logical_not(((z == 0) & (h == 1)) | is_root))
    def _():
        relay_factor(0, NCHUNK)

    @pl.when(h == 1)
    def _():
        finish_columns()

    @pl.when((q == 1) & (k != 0))
    def _():
        drain(brow, rf_r)

    @pl.when((h == 1) & (z != 0))
    def _():
        drain(coded, rf_r)
        decode_rows()

    winv = w[...]
    pcol = [nt(bcol[s], winv) for s in range(2)]

    def update(t, c):
        panel = nt(brow[t], winv)
        first = (k == 0) & (t == 0)
        for s in range(2):
            tile = asm[s, t] - nt(panel, pcol[s])
            tile = jnp.where(first, 0.0, tile)
            if s == 0:
                tile = jnp.where(q == 0, panel, tile)
            start = t * (TILE * 4) + 2 * s
            out[pl.ds(start, TILE, stride=4), :] = tile[:, :128]
            out[pl.ds(start + 1, TILE, stride=4), :] = tile[:, 128:]
        return c

    lax.fori_loop(0, TR, update, 0)

    @pl.when(is_root)
    def _():
        ii = lax.broadcasted_iota(jnp.int32, (TILE, TILE), 0)
        jj = lax.broadcasted_iota(jnp.int32, (TILE, TILE), 1)
        factor = jnp.where(ii >= jj, u_ref[...].T, 0.0)
        out[pl.ds(0, TILE, stride=4), :] = factor[:, :128]
        out[pl.ds(1, TILE, stride=4), :] = factor[:, 128:]

    for i in range(1, NX):
        drain(stage.at[0], ch_s.at[i])

    def each(count, view, sem):
        def one(i, c):
            drain(view, sem)
            return c
        lax.fori_loop(0, count, one, 0)

    @pl.when((q == 0) & (k != 0))
    def _():
        each(jnp.where(k == NCOL, OWNERS - 1, OWNERS), col_out.at[0], cs_s)

    each(NY - 1, col.at[:, 0:PIECE, :], cy_s)
    each(NX - 1, col.at[:, 0:GROUP, :], cx_s)

    @pl.when(((q == 0) & (k != 0)) | is_helper)
    def _():
        each(NZ - 1, coded.at[0], rs_s)
        each(NZ - 1, coded.at[0], ra_s)

    @pl.when((h == 0) & (z != 0))
    def _():
        each(NZ - 2, coded.at[0], ra_s)
        drain(coded, rf_s)

    @pl.when(q == 0)
    def _():
        drain(brow, rf_s)

    sent = (
        jnp.where((h == 1) & (y == 0) & (z == 0), NY - 1, 0)
        + jnp.where((h == 1) & (z == 0), NZ - 1, 0)
        + jnp.where((h == 1) & jnp.logical_not(is_helper), 1, 0)
        + jnp.where(is_root, NX, 0)
    )
    for i in range(NCHUNK):
        each(sent, part(i), w_s)


def local(front_tiles, child_tiles, target_rows, target_cols, live_counts):
    front = front_tiles.reshape(TR * TILE * 4, 128)
    child = child_tiles.reshape(SLOTS, TILE, TILE)
    hbm = pl.BlockSpec(memory_space=pltpu.HBM)
    dma = pltpu.SemaphoreType.DMA
    out = pl.pallas_call(
        kernel,
        out_shape=pltpu.VMEM(front.shape, F32),
        in_specs=[hbm] * 5,
        out_specs=pl.BlockSpec(memory_space=pltpu.VMEM),
        scratch_shapes=[
            pltpu.VMEM(front.shape, F32),
            pltpu.VMEM(child.shape, BF16),
            pltpu.SMEM((SLOTS,), jnp.int32),
            pltpu.SMEM((SLOTS,), jnp.int32),
            pltpu.SMEM((1,), jnp.int32),
            dma((5,)),
            pltpu.VMEM((NX, STAGE_ROWS, TILE), BF16),
            pltpu.VMEM((NX, STAGE_ROWS, TILE), BF16),
            pltpu.VMEM((2, TR, TILE, TILE), F32),
            pltpu.VMEM((TR, TILE, TILE), F32),
            pltpu.VMEM((NZ, CODED_ROWS, TILE), jnp.int16),
            pltpu.VMEM((OWNERS, 2 * PIECE, HALF), jnp.int16),
            pltpu.VMEM((2, 2 * PIECE, HALF), jnp.int16),
            pltpu.VMEM((2, 2 * TILE, HALF), jnp.int16),
            pltpu.VMEM((2, TILE, TILE), F32),
            pltpu.VMEM((TILE, TILE), F32),
            pltpu.VMEM((TILE, 2 * TILE), F32),
            pltpu.VMEM((TILE, TILE), F32),
            dma((NX,)), dma((NX,)),
            dma, dma((2,)),
            dma, dma,
            dma, dma((NX,)),
            dma, dma,
            dma, dma((NZ,)),
            dma, dma,
            dma, dma((NCHUNK,)),
            pltpu.SemaphoreType.REGULAR,
        ],
        compiler_params=pltpu.CompilerParams(
            collective_id=0, has_side_effects=True, vmem_limit_bytes=56 * 1024 * 1024
        ),
        cost_estimate=pl.CostEstimate(flops=11 * 2 * TILE**3, bytes_accessed=4 * 1024 * 1024, transcendentals=0),
        name="front_panel",
    )(front, child, target_rows.reshape(SLOTS), target_cols.reshape(SLOTS), live_counts.reshape(1))
    return out.reshape(front_tiles.shape)


def solution(mesh):
    placed = (
        P(None, ("cube", "row"), None, None, "col", None),
        P("cube", "row", "col", None, None, None),
        P("cube", "row", "col", None),
        P("cube", "row", "col", None),
        P("cube", "row", "col"),
    )
    return jax.shard_map(
        local,
        mesh=mesh,
        in_specs=placed,
        out_specs=P(None, ("cube", "row"), None, None, "col", None),
        check_vma=False,
    )
```
